256 devices in a mesh: elec: 32 (over z, y), cell: 8 (over x, core).
Axes of the slice: x: 4, y: 4, z: 8, core: 2. Of those that a mesh axis runs over, the one named last changes fastest.
Arguments:
- fields: bfloat16 [512, 3, 65536], P('elec', None, 'cell'), may hold values from -6 to 6
- cell_weight: float32 [65536], P('cell')
- resolution_basis: bfloat16 [65536, 512], P('cell')
- pattern: int32 [32, 4], P('elec'), may hold values from 0 to 1, as said below
- quadrupoles: int32 [2048, 4], P('elec'), may hold values from 0 to 511, as said below
Outputs:
- projection: float32 [512, 2048], P('cell', 'elec')
- design_gain: float32 [2048], P('elec')
The draws below stay inside these ranges and needn't reach their ends.
Inputs may be any that keep to these rules, and one draw needn't show every extreme that they name: `pattern`: row i is 1 for offsets below a count of 1 to 4 and 0 from there on; the count never reaches past the last block (32 - i at most), and some row has 4 ones. `quadrupoles`: A, B, M, N are four different electrodes. A and B lie in one block of 16 electrodes (electrode // 16); M and N lie together in that block or one of the next 3 blocks, at an offset that pattern marks 1 for A's block. Among the 64 candidates of one device (aligned blocks of rows), at most 4 have A in any one block, and on every device some electrode block holds exactly 4 of them.
All inputs are finite; a program needn't handle non-finite values.
Results may differ from the reference program's by a relative error of at most 0.0029.
Values may be sent and summed in bfloat16 or wider, within the bound.
A program may use at most 128 MiB of HBM per device.

```python
import math
import jax
import jax.numpy as jnp
from jax import lax

EL_DEV = 16
KB = 4
R = 512
Q_DEV = 64
BLOCKS = 32
E = 512
NC = 65536
Q = 2048
CAP = 4


def tile_plan(key):
    key_counts, key_heavy, key_quads = jax.random.split(key, 3)
    block_ids = jnp.arange(BLOCKS)
    counts = jax.random.randint(key_counts, (BLOCKS,), 1, KB + 1)
    heavy = jax.random.randint(key_heavy, (), 0, BLOCKS - KB + 1)
    counts = jnp.where(block_ids == heavy, KB, counts)
    counts = jnp.minimum(counts, BLOCKS - block_ids)
    pattern = (jnp.arange(KB)[None, :] < counts[:, None]).astype(jnp.int32)

    def one_device(index):
        keys = jax.random.split(jax.random.fold_in(key_quads, index), 6)
        crowded = jax.random.randint(keys[0], (), 0, BLOCKS)
        others = jnp.repeat(jnp.arange(BLOCKS - 1, dtype=jnp.int32), CAP)
        others = jax.random.permutation(keys[1], others)[:Q_DEV - CAP]
        others = others + (others >= crowded).astype(jnp.int32)
        owners = jnp.concatenate([jnp.full((CAP,), crowded, jnp.int32), others.astype(jnp.int32)])
        owners = jax.random.permutation(keys[2], owners)
        offsets = jax.random.randint(keys[3], (Q_DEV,), 0, 1 << 20) % counts[owners]
        starts = jax.random.randint(keys[4], (Q_DEV,), 0, EL_DEV)
        gaps = jax.random.randint(keys[5], (Q_DEV, 3), 0, 5) + 1
        spacing = jnp.concatenate([jnp.zeros((Q_DEV, 1), jnp.int32), jnp.cumsum(gaps, 1).astype(jnp.int32)], 1)
        local_index = (starts[:, None] + spacing) % EL_DEV
        sink_block = owners + offsets
        block_of = jnp.stack([owners, owners, sink_block, sink_block], 1)
        return (block_of * EL_DEV + local_index).astype(jnp.int32)
    quads = jax.vmap(one_device)(block_ids).reshape(Q, 4)
    return (pattern, quads)


def draw_pattern(key, part):
    pattern, quads = tile_plan(key)
    return pattern


def draw_quadrupoles(key, part):
    pattern, quads = tile_plan(key)
    return quads


def draw_cell_weight(key, part):
    key = jax.random.fold_in(key, 7)
    ramp = 1.0 + 2.0 * jnp.arange(NC, dtype=jnp.float32) / (NC - 1)
    spread = jnp.exp(jax.random.uniform(key, (NC,), jnp.float32, math.log(0.5), math.log(2.0)))
    return spread * ramp


def draw_resolution_basis(key, part):
    key = jax.random.fold_in(key, 9)
    column_scale = jnp.sqrt(1.0 + 2.0 * jnp.arange(R, dtype=jnp.float32) / (R - 1))
    values = jax.random.normal(key, (NC, R), jnp.float32)
    return (values * column_scale[None, :] / math.sqrt(NC)).astype(jnp.bfloat16)


def shard_levels(stream_key, extent, shards, low, high):
    def one(dim, shards_of):
        heights = jax.random.uniform(jax.random.fold_in(jax.random.fold_in(stream_key, 6), dim), (shards_of,), jnp.float32, low / len(shards), high / len(shards))
        return jnp.repeat(jnp.exp(heights), extent[dim] // shards_of).reshape((-1,) + (1,) * (len(extent) - dim - 1))

    level = one(*shards[0])
    for cut in shards[1:]:
        level = level * one(*cut)
    return level


def gaussian(key, shape, deviation, reach, pieces=(), kind=jnp.bfloat16):
    result = deviation * jax.random.normal(key, shape, jnp.float32)
    if pieces:
        result = result * shard_levels(key, shape, pieces, -0.22, 0.18)
    return jnp.clip(result, -reach, reach).astype(kind)


def setup_inputs(seed: int = 0) -> dict:
    key_list = jax.random.split(jax.random.key(seed), 6)
    fields = gaussian(key_list[0], (E, 3, NC), 1.0, 6.0, ((0, 32), (2, 8)))
    cell_weight = draw_cell_weight(jax.random.fold_in(key_list[5], 71), 0)
    resolution_basis = draw_resolution_basis(jax.random.fold_in(key_list[5], 71), 0)
    pattern = draw_pattern(jax.random.fold_in(key_list[5], 71), 0)
    quadrupoles = draw_quadrupoles(jax.random.fold_in(key_list[5], 71), 0)
    return {"fields": fields, "cell_weight": cell_weight, "resolution_basis": resolution_basis, "pattern": pattern, "quadrupoles": quadrupoles}


def pair_field(left_field, right_field, cell_weight):
    product = cell_weight * jnp.sum(left_field * right_field, axis=1)
    return lax.optimization_barrier(product.astype(jnp.bfloat16)).astype(jnp.float32)


def reference(fields, cell_weight, resolution_basis, pattern, quadrupoles):
    widened = fields.astype(jnp.float32)
    basis_wide = resolution_basis.astype(jnp.float32)
    owner_block = quadrupoles[:, 0] // EL_DEV
    offset = quadrupoles[:, 2] // EL_DEV - owner_block
    live_tile = pattern[owner_block, offset].astype(jnp.float32)

    def project(block_rows):
        source_a = widened[block_rows[:, 0]]
        source_b = widened[block_rows[:, 1]]
        sink_m = widened[block_rows[:, 2]]
        sink_n = widened[block_rows[:, 3]]
        sensitivity = pair_field(source_a, sink_m, cell_weight) - pair_field(source_a, sink_n, cell_weight)
        sensitivity = sensitivity - pair_field(source_b, sink_m, cell_weight) + pair_field(source_b, sink_n, cell_weight)
        return jnp.dot(sensitivity, basis_wide, precision=lax.Precision.HIGHEST)

    projected = lax.map(project, quadrupoles.reshape(Q // Q_DEV, Q_DEV, 4)).reshape(Q, R)
    projected = projected * live_tile[:, None]
    energy = jnp.sum(projected * projected, axis=1)
    return projected.T, jnp.log1p(energy / R)
```

```python
import functools

import jax
import jax.numpy as jnp
from jax import lax
from jax.experimental import pallas as pl
from jax.experimental.pallas import tpu as pltpu
from jax.sharding import PartitionSpec as P

NY = 4
NX = 4
CORES = 2
CAP = 4
MESH = pl.DeviceIdType.MESH


def kernel(
    sizes,
    fields,
    weight,
    basis,
    pattern,
    quads,
    projection,
    energy,
    rows,
    basis_here,
    basis_turned,
    weight_here,
    asked,
    onehot,
    partial,
    from_core,
    core_sum,
    from_x,
    x_sum,
    from_y,
    to_z,
    from_z,
    own_energy,
    energies,
    local_sem,
    ask_send,
    ask_y,
    ask_z_send,
    ask_z,
    fy_send,
    fy_recv,
    fz_send,
    fz_recv,
    core_send,
    core_recv,
    x_send,
    x_recv,
    y_send,
    y_recv,
    z_send,
    z_recv,
    e_send,
    e_recv,
):
    nz, block, cells, chunks, slots, rank, here = sizes
    quarter = cells // NY
    width = quarter // chunks
    half = NY * nz * NY * slots
    elec = lax.axis_index("elec")
    cell = lax.axis_index("cell")
    z, y = lax.div(elec, NY), lax.rem(elec, NY)
    x, core = lax.div(cell, CORES), lax.rem(cell, CORES)

    def turn(value, step, size):
        return lax.rem(value + step, size)

    def at_y(other):
        return (z * NY + other, cell)

    def at_z(other):
        return (other * NY + y, cell)

    def at_cell(other):
        return (elec, other)

    def remote(src, dst, send, recv, device):
        return pltpu.make_async_remote_copy(
            src_ref=src, dst_ref=dst, send_sem=send, recv_sem=recv, device_id=device, device_id_type=MESH
        )

    load_basis = pltpu.make_async_copy(basis.at[pl.ds(y * quarter, quarter)], basis_here, local_sem.at[0])
    load_weight = pltpu.make_async_copy(weight.at[:, pl.ds(y * quarter, quarter)], weight_here, local_sem.at[1])
    load_own = pltpu.make_async_copy(
        fields.at[:, :, pl.ds(y * quarter, quarter)], rows.at[:, pl.ds(y * block, block), :], local_sem.at[2]
    )
    load_basis.start()
    load_weight.start()
    load_own.start()

    with jax.named_scope("barrier"):
        barrier = pltpu.get_barrier_semaphore()
        for d in range(1, NY):
            pl.semaphore_signal(barrier, inc=1, device_id=at_y(turn(y, d, NY)), device_id_type=MESH)
        for d in range(1, nz):
            pl.semaphore_signal(barrier, inc=1, device_id=at_z(turn(z, d, nz)), device_id_type=MESH)
        for d in range(1, NX * CORES):
            pl.semaphore_signal(barrier, inc=1, device_id=at_cell(turn(cell, d, NX * CORES)), device_id_type=MESH)
        pads = (NY * 2 - 1) * block
        rows[:, pads:, :] = jnp.zeros((3, rows.shape[1] - pads, quarter), jnp.bfloat16)
        asked[y, z] = jnp.full(asked.shape[2:], -1, jnp.int32)
        asked[y, z, 0:4, 0:here] = quads[...]
        asked[y, z, 4:5, 0 : pattern.shape[1]] = pattern[...]
        pl.semaphore_wait(barrier, NY - 1 + nz - 1 + NX * CORES - 1)

    ask_copies = []
    for d in range(1, NY):
        ask_copies.append(
            remote(asked.at[y, z], asked.at[y, z], ask_send.at[d], ask_y.at[d], at_y(turn(y, d, NY)))
        )
        ask_copies[-1].start()

    def y_copy(c, d):
        target = turn(y, d, NY)
        return remote(
            fields.at[:, :, pl.ds(target * quarter + c * width, width)],
            rows.at[:, pl.ds(y * block, block), pl.ds(c * width, width)],
            fy_send.at[c, d],
            fy_recv.at[c, d],
            at_y(target),
        )

    above = at_z(turn(z, nz - 1, nz))

    def z_own(c):
        return remote(
            fields.at[:, :, pl.ds(y * quarter + c * width, width)],
            rows.at[:, pl.ds((NY + y) * block, block), pl.ds(c * width, width)],
            fz_send.at[c, y],
            fz_recv.at[c, y],
            above,
        )

    def z_pass(c, b):
        return remote(
            rows.at[:, pl.ds(b * block, block), pl.ds(c * width, width)],
            rows.at[:, pl.ds((NY + b) * block, block), pl.ds(c * width, width)],
            fz_send.at[c, b],
            fz_recv.at[c, b],
            above,
        )

    for c in range(chunks):
        for d in (2, 1, 3):
            y_copy(c, d).start()

        @pl.when(y < NY - 1)
        def _(c=c):
            z_own(c).start()

    with jax.named_scope("ask"):
        for d in range(1, NY):
            ask_copies[d - 1].wait_recv()
        for d in range(1, nz):
            ask_copies.append(
                remote(asked.at[:, z], asked.at[:, z], ask_z_send.at[d], ask_z.at[d], at_z(turn(z, d, nz)))
            )
            ask_copies[-1].start()

    with jax.named_scope("turn_basis"):
        load_basis.wait()
        basis_turned[...] = basis_here[...].T
        load_weight.wait()
        load_own.wait()

    def forward(c):
        with jax.named_scope("forward"):
            for d in (1, 3, 2):
                y_copy(c, d).wait_recv()
                source = turn(y, NY - d, NY)

                @pl.when(source < NY - 1)
                def _(c=c, source=source):
                    z_pass(c, source).start()

    forward(0)

    lanes = asked.shape[-1]
    earlier = (
        lax.broadcasted_iota(jnp.int32, (lanes, lanes), 0) < lax.broadcasted_iota(jnp.int32, (lanes, lanes), 1)
    ).astype(jnp.bfloat16)

    def slot_match(in_block, slot):
        before = jnp.dot(in_block.astype(jnp.bfloat16), earlier, preferred_element_type=jnp.float32)
        return jnp.logical_and(in_block > 0.5, before == slot.astype(jnp.float32))

    with jax.named_scope("onehot"):
        for d in range(1, nz):
            ask_copies[NY - 1 + d - 1].wait_recv()
        devices = NY * nz
        group = NY * slots

        def wide(row):
            line = asked[:, :, row, :].reshape(devices, 1, lanes)
            return jnp.broadcast_to(line, (devices, group, lanes))

        inner = lax.broadcasted_iota(jnp.int32, (devices, group, lanes), 1)
        a_wide = wide(0)
        in_block = jnp.where(lax.shift_right_arithmetic(a_wide, 4) == z * NY + lax.div(inner, slots), 1.0, 0.0)
        in_block = in_block.reshape(half, lanes)
        slot = lax.rem(inner, slots).reshape(half, lanes)
        match = slot_match(in_block, slot)
        lane = lax.broadcasted_iota(jnp.int32, (half, lanes), 1)

        def local(row):
            value = (wide(row) - (z * NY * block - 1)).reshape(half, lanes).astype(jnp.float32)
            return jnp.sum(jnp.where(match, value, 0.0), axis=1, keepdims=True)

        a, b, m, n = (local(row).astype(jnp.int32) for row in range(4))
        offset = lax.shift_right_arithmetic(m - 1, 4) - lax.shift_right_arithmetic(a - 1, 4)
        used = asked[:, z, 4, :].reshape(NY, 1, lanes)
        used = jnp.broadcast_to(used, (NY, slots, lanes)).reshape(1, group, lanes)
        used = jnp.broadcast_to(used, (devices, group, lanes)).reshape(half, lanes)
        live = jnp.sum(jnp.where(lane == offset, used.astype(jnp.float32), 0.0), axis=1, keepdims=True)
        one = jnp.where(lane == a - 1, 1.0, 0.0) - jnp.where(lane == b - 1, 1.0, 0.0)
        onehot[0:half] = (live * one).astype(jnp.bfloat16)
        two = jnp.where(lane == m - 1, 1.0, 0.0) - jnp.where(lane == n - 1, 1.0, 0.0)
        onehot[half : 2 * half] = two.astype(jnp.bfloat16)

    def compute(c):
        with jax.named_scope("gather_fields"):
            for b in range(NY - 1):
                z_pass(c, b).wait_recv()
        with jax.named_scope("sensitivity"):
            span = slice(c * width, (c + 1) * width)
            total = None
            for component in range(3):
                picked = jnp.dot(onehot[...], rows[component, :, span], preferred_element_type=jnp.float32)
                term = picked[:half] * picked[half:]
                total = term if total is None else total + term
            sensitivity = (total * weight_here[:, span]).astype(jnp.bfloat16)
            part = lax.dot_general(
                basis_turned[:, span],
                sensitivity,
                (((1,), (1,)), ((), ())),
                preferred_element_type=jnp.float32,
            ).reshape(partial.shape)
            partial[...] = part if c == 0 else partial[...] + part

    for c in range(chunks):
        if c + 1 < chunks:
            forward(c + 1)
        compute(c)

    with jax.named_scope("sum_core"):
        sibling = at_cell(x * CORES + (1 - core))
        for d in (2, 1, 3, 0):
            target = turn(x, d, NX)
            remote(
                partial.at[target, 1 - core], from_core.at[target], core_send.at[d], core_recv.at[d], sibling
            ).start()

    def core_copy(d):
        target = turn(x, d, NX)
        return remote(
            partial.at[target, 1 - core], from_core.at[target], core_send.at[d], core_recv.at[d], sibling
        )

    def x_copy(d):
        target = turn(x, d, NX)
        return remote(
            core_sum.at[target], from_x.at[d], x_send.at[d], x_recv.at[d], at_cell(target * CORES + core)
        )

    with jax.named_scope("sum_x"):
        for d in (2, 1, 3, 0):
            target = turn(x, d, NX)
            core_copy(d).wait_recv()
            core_sum[target] = partial[target, core] + from_core[target]
            if d:
                x_copy(d).start()
        total = core_sum[x]
        for d in (1, 3, 2):
            x_copy(d).wait_recv()
            total = total + from_x[d]

    lane_group = nz * NY * slots
    with jax.named_scope("sum_y"):
        for other in range(NY):
            x_sum[other] = total[:, other * lane_group : (other + 1) * lane_group]

        def y_sum_copy(d):
            target = turn(y, d, NY)
            return remote(x_sum.at[target], from_y.at[d], y_send.at[d], y_recv.at[d], at_y(target))

        for d in (2, 1, 3):
            y_sum_copy(d).start()
        total = x_sum[y]
        for d in (1, 3, 2):
            y_sum_copy(d).wait_recv()
            total = total + from_y[d]

    with jax.named_scope("return_z"):
        part = total.shape[0]
        spread = jnp.concatenate([total, jnp.zeros((lanes - part, lane_group), jnp.float32)], axis=0)
        to_z[...] = spread.T.reshape(to_z.shape)

        def z_copy(d):
            target = turn(z, d, nz)
            return remote(to_z.at[target], from_z.at[z], z_send.at[d], z_recv.at[d], at_z(target))

        for d in range(1, nz):
            z_copy(d).start()
        from_z[z] = to_z[z]
        slot_row = lax.broadcasted_iota(jnp.int32, (lane_group, lanes), 0)
        mine = jnp.broadcast_to(lax.shift_right_arithmetic(asked[y, z, 0:1, :], 4), (lane_group, lanes))
        own_block = jnp.where(mine == lax.div(slot_row, slots), 1.0, 0.0)
        own_match = slot_match(own_block, lax.rem(slot_row, slots)).astype(jnp.float32)
        for d in range(1, nz):
            z_copy(d).wait_recv()
        returned = from_z[...].reshape(lane_group, lanes).T
        own = jnp.dot(
            returned, own_match, precision=lax.Precision.HIGHEST, preferred_element_type=jnp.float32
        )
        projection[...] = own[:part, :here]

    with jax.named_scope("energies"):
        own_energy[...] = jnp.broadcast_to(jnp.sum(own * own, axis=0, keepdims=True), own_energy.shape)

        def e_copy(d):
            target = turn(cell, d, NX * CORES)
            return remote(own_energy, energies.at[d], e_send.at[d], e_recv.at[d], at_cell(target))

        for d in range(1, NX * CORES):
            e_copy(d).start()
        total = own_energy[...]
        for d in range(1, NX * CORES):
            e_copy(d).wait_recv()
            total = total + energies[d]
        energy[...] = total[0:1, :here]

    with jax.named_scope("drain"):
        for copy in ask_copies:
            copy.wait_send()
        for c in range(chunks):
            for d in range(1, NY):
                y_copy(c, d).wait_send()
            for b in range(NY - 1):
                z_pass(c, b).wait_send()
        for d in range(NX):
            core_copy(d).wait_send()
        for d in range(1, NX):
            x_copy(d).wait_send()
        for d in range(1, NY):
            y_sum_copy(d).wait_send()
        for d in range(1, nz):
            z_copy(d).wait_send()
        for d in range(1, NX * CORES):
            e_copy(d).wait_send()


def per_device(fields, cell_weight, resolution_basis, pattern, quadrupoles, chunks=4):
    block, components, cells = fields.shape
    rank = resolution_basis.shape[1]
    here = quadrupoles.shape[0]
    nz = lax.axis_size("elec") // NY
    quarter = cells // NY
    part = rank // (NX * CORES)
    lanes = 128
    slots = CAP
    half = nz * NY * NY * slots
    group = nz * NY * slots
    held = 2 * NY * block
    dma = pltpu.SemaphoreType.DMA
    vmem = pl.BlockSpec(memory_space=pltpu.VMEM)
    anywhere = pl.BlockSpec(memory_space=pl.ANY)
    sizes = (nz, block, cells, chunks, slots, rank, here)
    projection, energy = pl.pallas_call(
        functools.partial(kernel, sizes),
        out_shape=(
            jax.ShapeDtypeStruct((part, here), jnp.float32),
            jax.ShapeDtypeStruct((1, here), jnp.float32),
        ),
        in_specs=[anywhere, anywhere, anywhere, vmem, vmem],
        out_specs=(vmem, vmem),
        scratch_shapes=[
            pltpu.VMEM((components, held, quarter), jnp.bfloat16),
            pltpu.VMEM((quarter, rank), jnp.bfloat16),
            pltpu.VMEM((rank, quarter), jnp.bfloat16),
            pltpu.VMEM((1, quarter), jnp.float32),
            pltpu.VMEM((NY, nz, 8, lanes), jnp.int32),
            pltpu.VMEM((2 * half, lanes), jnp.bfloat16),
            pltpu.VMEM((NX, CORES, part, half), jnp.float32),
            pltpu.VMEM((NX, part, half), jnp.float32),
            pltpu.VMEM((NX, part, half), jnp.float32),
            pltpu.VMEM((NX, part, half), jnp.float32),
            pltpu.VMEM((NY, part, group), jnp.float32),
            pltpu.VMEM((NY, part, group), jnp.float32),
            pltpu.VMEM((nz, NY * slots, lanes), jnp.float32),
            pltpu.VMEM((nz, NY * slots, lanes), jnp.float32),
            pltpu.VMEM((8, lanes), jnp.float32),
            pltpu.VMEM((NX * CORES, 8, lanes), jnp.float32),
            dma((3,)),
            dma((NY,)),
            dma((NY,)),
            dma((nz,)),
            dma((nz,)),
            dma((chunks, NY)),
            dma((chunks, NY)),
            dma((chunks, NY)),
            dma((chunks, NY)),
            dma((NX,)),
            dma((NX,)),
            dma((NX,)),
            dma((NX,)),
            dma((NY,)),
            dma((NY,)),
            dma((nz,)),
            dma((nz,)),
            dma((NX * CORES,)),
            dma((NX * CORES,)),
        ],
        compiler_params=pltpu.CompilerParams(
            collective_id=0, has_side_effects=True, vmem_limit_bytes=48 * 1024 * 1024
        ),
    )(
        fields.transpose(1, 0, 2),
        cell_weight.reshape(1, cells),
        resolution_basis,
        pattern,
        quadrupoles.T,
    )
    return projection, jnp.log1p(energy.reshape(here) / rank)


def solution(mesh):
    placed = (P("elec", None, "cell"), P("cell"), P("cell", None), P("elec", None), P("elec", None))
    return jax.shard_map(
        per_device,
        mesh=mesh,
        in_specs=placed,
        out_specs=(P("cell", "elec"), P("elec")),
        check_vma=False,
    )
```

```python
import functools

import jax
import jax.numpy as jnp
from jax import lax
from jax.experimental import pallas as pl
from jax.experimental.pallas import tpu as pltpu
from jax.sharding import PartitionSpec as P

NY = 4
NX = 4
CORES = 2
CAP = 4
MESH = pl.DeviceIdType.MESH


def kernel(
    sizes,
    fields,
    weight,
    basis,
    pattern,
    quads,
    projection,
    energy,
    rows,
    basis_here,
    weight_here,
    asked,
    onehot,
    pick,
    partial,
    from_core,
    own_sum,
    to_y,
    from_y,
    to_z,
    from_z,
    mine,
    from_x,
    turned,
    from_sibling,
    own_energy,
    sibling_energy,
    pattern_here,
    quads_here,
    local_sem,
    ask_send,
    ask_y,
    ask_z_send,
    ask_z,
    fy_send,
    fy_recv,
    fz_send,
    fz_recv,
    core_send,
    core_recv,
    x_send,
    x_recv,
    y_send,
    y_recv,
    z_send,
    z_recv,
    last_send,
    last_recv,
):
    nz, block, cells, chunks, slots, rank, here = sizes
    quarter = cells // NY
    width = quarter // chunks
    lane_group = nz * NY * slots
    half = NY * lane_group
    elec = lax.axis_index("elec")
    cell = lax.axis_index("cell")
    z, y = lax.div(elec, NY), lax.rem(elec, NY)
    x, core = lax.div(cell, CORES), lax.rem(cell, CORES)

    def turn(value, step, size):
        return lax.rem(value + step, size)

    def at_y(other):
        return (z * NY + other, cell)

    def at_z(other):
        return (other * NY + y, cell)

    def at_cell(other):
        return (elec, other)

    sibling = at_cell(x * CORES + (1 - core))

    def remote(src, dst, send, recv, device):
        return pltpu.make_async_remote_copy(
            src_ref=src, dst_ref=dst, send_sem=send, recv_sem=recv, device_id=device, device_id_type=MESH
        )

    load_basis = pltpu.make_async_copy(basis.at[pl.ds(y * quarter, quarter)], basis_here, local_sem.at[0])
    load_weight = pltpu.make_async_copy(weight.at[:, pl.ds(y * quarter, quarter)], weight_here, local_sem.at[1])
    load_own = pltpu.make_async_copy(
        fields.at[:, :, pl.ds(y * quarter, quarter)], rows.at[:, pl.ds(y * block, block), :], local_sem.at[2]
    )
    load_quads = pltpu.make_async_copy(quads, quads_here, local_sem.at[3])
    load_pattern = pltpu.make_async_copy(pattern, pattern_here, local_sem.at[4])
    load_quads.start()
    load_pattern.start()
    load_basis.start()
    load_weight.start()
    load_own.start()

    with jax.named_scope("barrier"):
        barrier = pltpu.get_barrier_semaphore()
        for d in range(1, nz):
            pl.semaphore_signal(barrier, inc=1, device_id=at_z(turn(z, d, nz)), device_id_type=MESH)
        for d in range(1, NY):
            pl.semaphore_signal(barrier, inc=1, device_id=at_y(turn(y, d, NY)), device_id_type=MESH)
        for d in range(1, NX):
            other = at_cell(turn(x, d, NX) * CORES + core)
            pl.semaphore_signal(barrier, inc=1, device_id=other, device_id_type=MESH)
        pl.semaphore_signal(barrier, inc=1, device_id=sibling, device_id_type=MESH)
        pads = (NY * 2 - 1) * block
        rows[:, pads:, :] = jnp.zeros((3, rows.shape[1] - pads, quarter), jnp.bfloat16)
        asked[y, z] = jnp.full(asked.shape[2:], -1, jnp.int32)
        load_quads.wait()
        load_pattern.wait()
        asked[y, z, 0:4, 0:here] = quads_here[...]
        asked[y, z, 4:5, 0 : pattern.shape[1]] = pattern_here[...]
        pl.semaphore_wait(barrier, NY - 1 + nz - 1 + NX - 1 + CORES - 1)

    ask_copies = []
    for d in range(1, NY):
        ask_copies.append(
            remote(asked.at[y, z], asked.at[y, z], ask_send.at[d], ask_y.at[d], at_y(turn(y, d, NY)))
        )
        ask_copies[-1].start()

    def y_copy(c, d):
        target = turn(y, d, NY)
        return remote(
            fields.at[:, :, pl.ds(target * quarter + c * width, width)],
            rows.at[:, pl.ds(y * block, block), pl.ds(c * width, width)],
            fy_send.at[c, d],
            fy_recv.at[c, d],
            at_y(target),
        )

    above = at_z(turn(z, nz - 1, nz))

    def z_own(c):
        return remote(
            fields.at[:, :, pl.ds(y * quarter + c * width, width)],
            rows.at[:, pl.ds((NY + y) * block, block), pl.ds(c * width, width)],
            fz_send.at[c, y],
            fz_recv.at[c, y],
            above,
        )

    def z_pass(c, b):
        return remote(
            rows.at[:, pl.ds(b * block, block), pl.ds(c * width, width)],
            rows.at[:, pl.ds((NY + b) * block, block), pl.ds(c * width, width)],
            fz_send.at[c, b],
            fz_recv.at[c, b],
            above,
        )

    for c in range(chunks):
        for d in (2, 1, 3):
            y_copy(c, d).start()

        @pl.when(y < NY - 1)
        def _(c=c):
            z_own(c).start()

    with jax.named_scope("ask"):
        for d in range(1, NY):
            ask_copies[d - 1].wait_recv()
        for d in range(1, nz):
            ask_copies.append(
                remote(asked.at[:, z], asked.at[:, z], ask_z_send.at[d], ask_z.at[d], at_z(turn(z, d, nz)))
            )
            ask_copies[-1].start()

    def forward(c):
        with jax.named_scope("forward"):
            for d in (1, 3, 2):
                y_copy(c, d).wait_recv()
                source = turn(y, NY - d, NY)

                @pl.when(source < NY - 1)
                def _(c=c, source=source):
                    z_pass(c, source).start()

    load_own.wait()
    forward(0)

    lanes = asked.shape[-1]
    earlier = (
        lax.broadcasted_iota(jnp.int32, (lanes, lanes), 0) < lax.broadcasted_iota(jnp.int32, (lanes, lanes), 1)
    ).astype(jnp.bfloat16)

    def slot_match(in_block, slot):
        before = jnp.dot(in_block.astype(jnp.bfloat16), earlier, preferred_element_type=jnp.float32)
        return jnp.logical_and(in_block > 0.5, before == slot.astype(jnp.float32))

    with jax.named_scope("onehot"):
        for d in range(1, nz):
            ask_copies[NY - 1 + d - 1].wait_recv()
        devices = NY * nz
        group = NY * slots

        def wide(row):
            line = asked[:, :, row, :].reshape(devices, 1, lanes)
            return jnp.broadcast_to(line, (devices, group, lanes))

        inner = lax.broadcasted_iota(jnp.int32, (devices, group, lanes), 1)
        a_wide = wide(0)
        in_block = jnp.where(lax.shift_right_arithmetic(a_wide, 4) == z * NY + lax.div(inner, slots), 1.0, 0.0)
        in_block = in_block.reshape(half, lanes)
        slot = lax.rem(inner, slots).reshape(half, lanes)
        match = slot_match(in_block, slot)
        lane = lax.broadcasted_iota(jnp.int32, (half, lanes), 1)

        def local(row):
            value = (wide(row) - (z * NY * block - 1)).reshape(half, lanes).astype(jnp.float32)
            return jnp.sum(jnp.where(match, value, 0.0), axis=1, keepdims=True)

        a, b, m, n = (local(row).astype(jnp.int32) for row in range(4))
        offset = lax.shift_right_arithmetic(m - 1, 4) - lax.shift_right_arithmetic(a - 1, 4)
        used = asked[:, z, 4, :].reshape(NY, 1, lanes)
        used = jnp.broadcast_to(used, (NY, slots, lanes)).reshape(1, group, lanes)
        used = jnp.broadcast_to(used, (devices, group, lanes)).reshape(half, lanes)
        live = jnp.sum(jnp.where(lane == offset, used.astype(jnp.float32), 0.0), axis=1, keepdims=True)
        one = jnp.where(lane == a - 1, 1.0, 0.0) - jnp.where(lane == b - 1, 1.0, 0.0)
        onehot[0:half] = (live * one).astype(jnp.bfloat16)
        two = jnp.where(lane == m - 1, 1.0, 0.0) - jnp.where(lane == n - 1, 1.0, 0.0)
        onehot[half : 2 * half] = two.astype(jnp.bfloat16)

        slot_row = lax.broadcasted_iota(jnp.int32, (lane_group, lanes), 0)
        own_a = jnp.broadcast_to(lax.shift_right_arithmetic(asked[y, z, 0:1, :], 4), (lane_group, lanes))
        own_block = jnp.where(own_a == lax.div(slot_row, slots), 1.0, 0.0)
        own_match = slot_match(own_block, lax.rem(slot_row, slots)).astype(jnp.float32)
        pick[...] = own_match.T[:here].astype(jnp.bfloat16)
        load_basis.wait()
        load_weight.wait()

    def compute(c):
        with jax.named_scope("gather_fields"):
            for b in range(NY - 1):
                z_pass(c, b).wait_recv()
        with jax.named_scope("sensitivity"):
            span = slice(c * width, (c + 1) * width)
            total = None
            for component in range(3):
                picked = jnp.dot(onehot[...], rows[component, :, span], preferred_element_type=jnp.float32)
                term = picked[:half] * picked[half:]
                total = term if total is None else total + term
            sensitivity = total * weight_here[:, span]
            high = sensitivity.astype(jnp.bfloat16)
            low = (sensitivity - high.astype(jnp.float32)).astype(jnp.bfloat16)
            part = jnp.dot(high, basis_here[span, :], preferred_element_type=jnp.float32)
            part = part + jnp.dot(low, basis_here[span, :], preferred_element_type=jnp.float32)
            part = part.reshape(partial.shape)
            partial[...] = part if c == 0 else partial[...] + part

    for c in range(chunks):
        if c + 1 < chunks:
            forward(c + 1)
        compute(c)

    def own_half(other):
        return pl.ds(pl.multiple_of(other * (rank // CORES), 128), rank // CORES)

    def core_copy(d):
        target = turn(y, d, NY)
        return remote(
            partial.at[target, :, own_half(1 - core)],
            from_core.at[target],
            core_send.at[d],
            core_recv.at[d],
            sibling,
        )

    def y_sum_copy(d):
        target = turn(y, d, NY)
        return remote(to_y.at[target], from_y.at[d], y_send.at[d], y_recv.at[d], at_y(target))

    with jax.named_scope("sum_core"):
        for d in (2, 1, 3, 0):
            core_copy(d).start()
        for d in (2, 1, 3, 0):
            target = turn(y, d, NY)
            core_copy(d).wait_recv()
            summed = partial[target, :, own_half(core)] + from_core[target]
            if d:
                to_y[target] = summed.astype(jnp.bfloat16)
                y_sum_copy(d).start()
            else:
                own_sum[...] = summed

    with jax.named_scope("sum_y"):
        total = own_sum[...]
        for d in (1, 3, 2):
            y_sum_copy(d).wait_recv()
            total = total + from_y[d].astype(jnp.float32)

    def z_copy(d):
        target = turn(z, d, nz)
        return remote(to_z.at[target], from_z.at[z], z_send.at[d], z_recv.at[d], at_z(target))

    with jax.named_scope("return_z"):
        to_z[...] = total.astype(jnp.bfloat16).reshape(to_z.shape)
        for d in (4, 3, 5, 2, 6, 1, 7):
            if d < nz:
                z_copy(d).start()
        from_z[z] = to_z[z]
        for d in range(1, nz):
            z_copy(d).wait_recv()
        returned = from_z[...].reshape(lane_group, rank // CORES)
        mine[...] = jnp.dot(pick[...], returned, preferred_element_type=jnp.float32).astype(jnp.bfloat16)

    def x_copy(d):
        target = turn(x, d, NX)
        return remote(mine, from_x.at[d], x_send.at[d], x_recv.at[d], at_cell(target * CORES + core))

    with jax.named_scope("sum_x"):
        for d in (2, 1, 3):
            x_copy(d).start()
        total = mine[...].astype(jnp.float32)
        for d in (1, 3, 2):
            x_copy(d).wait_recv()
            total = total + from_x[d].astype(jnp.float32)
        total = jnp.concatenate([total, jnp.zeros((lanes - here, rank // CORES), jnp.float32)], axis=0).T
        turned[...] = total
        own_energy[...] = jnp.broadcast_to(jnp.sum(total * total, axis=0, keepdims=True), own_energy.shape)

    part = rank // (NX * CORES)
    chip_rows = lax.rem(x * CORES * part, rank // CORES)
    last = [
        remote(
            turned.at[pl.ds(pl.multiple_of(chip_rows + (1 - core) * part, 8), part)],
            from_sibling,
            last_send.at[0],
            last_recv.at[0],
            sibling,
        ),
        remote(own_energy, sibling_energy, last_send.at[1], last_recv.at[1], sibling),
    ]
    with jax.named_scope("cores"):
        for copy in last:
            copy.start()
        for copy in last:
            copy.wait_recv()
        kept = turned[pl.ds(pl.multiple_of(chip_rows + core * part, 8), part)]
        holder = lax.div(x * CORES * part, rank // CORES)
        chosen = jnp.where(holder == core, kept, from_sibling[...])
        projection[...] = chosen[:, :here]
        energy[...] = (own_energy[...] + sibling_energy[...])[0:1, :here]

    with jax.named_scope("drain"):
        for copy in ask_copies:
            copy.wait_send()
        for c in range(chunks):
            for d in range(1, NY):
                y_copy(c, d).wait_send()
            for b in range(NY - 1):
                z_pass(c, b).wait_send()
        for d in range(NY):
            core_copy(d).wait_send()
        for d in range(1, NY):
            y_sum_copy(d).wait_send()
        for d in range(1, nz):
            z_copy(d).wait_send()
        for d in range(1, NX):
            x_copy(d).wait_send()
        for copy in last:
            copy.wait_send()


def per_device(fields, cell_weight, resolution_basis, pattern, quadrupoles, chunks=4):
    block, components, cells = fields.shape
    rank = resolution_basis.shape[1]
    here = quadrupoles.shape[0]
    nz = lax.axis_size("elec") // NY
    quarter = cells // NY
    part = rank // (NX * CORES)
    lanes = 128
    slots = CAP
    half = nz * NY * NY * slots
    group = nz * NY * slots
    held = 2 * NY * block
    dma = pltpu.SemaphoreType.DMA
    vmem = pl.BlockSpec(memory_space=pltpu.VMEM)
    anywhere = pl.BlockSpec(memory_space=pl.ANY)
    sizes = (nz, block, cells, chunks, slots, rank, here)
    projection, energy = pl.pallas_call(
        functools.partial(kernel, sizes),
        out_shape=(
            jax.ShapeDtypeStruct((part, here), jnp.float32),
            jax.ShapeDtypeStruct((1, here), jnp.float32),
        ),
        in_specs=[anywhere] * 5,
        out_specs=(vmem, vmem),
        scratch_shapes=[
            pltpu.VMEM((components, held, quarter), jnp.bfloat16),
            pltpu.VMEM((quarter, rank), jnp.bfloat16),
            pltpu.VMEM((1, quarter), jnp.float32),
            pltpu.VMEM((NY, nz, 8, lanes), jnp.int32),
            pltpu.VMEM((2 * half, lanes), jnp.bfloat16),
            pltpu.VMEM((here, group), jnp.bfloat16),
            pltpu.VMEM((NY, group, rank), jnp.float32),
            pltpu.VMEM((NY, group, rank // CORES), jnp.float32),
            pltpu.VMEM((group, rank // CORES), jnp.float32),
            pltpu.VMEM((NY, group, rank // CORES), jnp.bfloat16),
            pltpu.VMEM((NY, group, rank // CORES), jnp.bfloat16),
            pltpu.VMEM((nz, NY * slots, rank // CORES), jnp.bfloat16),
            pltpu.VMEM((nz, NY * slots, rank // CORES), jnp.bfloat16),
            pltpu.VMEM((here, rank // CORES), jnp.bfloat16),
            pltpu.VMEM((NX, here, rank // CORES), jnp.bfloat16),
            pltpu.VMEM((rank // CORES, lanes), jnp.float32),
            pltpu.VMEM((part, lanes), jnp.float32),
            pltpu.VMEM((8, lanes), jnp.float32),
            pltpu.VMEM((8, lanes), jnp.float32),
            pltpu.VMEM((1, pattern.shape[1]), jnp.int32),
            pltpu.VMEM((4, here), jnp.int32),
            dma((5,)),
            dma((NY,)),
            dma((NY,)),
            dma((nz,)),
            dma((nz,)),
            dma((chunks, NY)),
            dma((chunks, NY)),
            dma((chunks, NY)),
            dma((chunks, NY)),
            dma((NX,)),
            dma((NX,)),
            dma((NX,)),
            dma((NX,)),
            dma((NY,)),
            dma((NY,)),
            dma((nz,)),
            dma((nz,)),
            dma((2,)),
            dma((2,)),
        ],
        compiler_params=pltpu.CompilerParams(
            collective_id=0, has_side_effects=True, vmem_limit_bytes=60 * 1024 * 1024
        ),
    )(
        fields.transpose(1, 0, 2),
        cell_weight.reshape(1, cells),
        resolution_basis,
        pattern,
        quadrupoles.T,
    )
    return projection, jnp.log1p(energy.reshape(here) / rank)


def solution(mesh):
    placed = (P("elec", None, "cell"), P("cell"), P("cell", None), P("elec", None), P("elec", None))
    return jax.shard_map(
        per_device,
        mesh=mesh,
        in_specs=placed,
        out_specs=(P("cell", "elec"), P("elec")),
        check_vma=False,
    )
```

```python
import functools

import jax
import jax.numpy as jnp
from jax import lax
from jax.experimental import pallas as pl
from jax.experimental.pallas import tpu as pltpu
from jax.sharding import PartitionSpec as P

NY = 4
NX = 4
CORES = 2
CAP = 4
MESH = pl.DeviceIdType.MESH


def kernel(
    sizes,
    fields,
    weight,
    basis,
    pattern,
    quads,
    projection,
    energy,
    rows,
    basis_here,
    weight_here,
    asked,
    used,
    onehot,
    pick,
    partial,
    from_core,
    own_sum,
    to_y,
    from_y,
    to_z,
    from_z,
    mine,
    from_x,
    turned,
    from_sibling,
    own_energy,
    sibling_energy,
    pattern_here,
    quads_here,
    local_sem,
    use_send,
    use_recv,
    ask_send,
    ask_y,
    ask_z_send,
    ask_z,
    fy_send,
    fy_recv,
    fz_send,
    fz_recv,
    core_send,
    core_recv,
    x_send,
    x_recv,
    y_send,
    y_recv,
    z_send,
    z_recv,
    last_send,
    last_recv,
):
    nz, block, cells, chunks, ahead, early, slots, rank, here = sizes
    quarter = cells // NY
    width = quarter // chunks
    lane_group = nz * NY * slots
    half = NY * lane_group
    elec = lax.axis_index("elec")
    cell = lax.axis_index("cell")
    z, y = lax.div(elec, NY), lax.rem(elec, NY)
    x, core = lax.div(cell, CORES), lax.rem(cell, CORES)

    def turn(value, step, size):
        return lax.rem(value + step, size)

    def at_y(other):
        return (z * NY + other, cell)

    def at_z(other):
        return (other * NY + y, cell)

    def at_cell(other):
        return (elec, other)

    sibling = at_cell(x * CORES + (1 - core))

    def remote(src, dst, send, recv, device):
        return pltpu.make_async_remote_copy(
            src_ref=src, dst_ref=dst, send_sem=send, recv_sem=recv, device_id=device, device_id_type=MESH
        )

    load_basis = pltpu.make_async_copy(basis.at[pl.ds(y * quarter, quarter)], basis_here, local_sem.at[0])
    load_weight = pltpu.make_async_copy(weight.at[:, pl.ds(y * quarter, quarter)], weight_here, local_sem.at[1])
    load_own = pltpu.make_async_copy(
        fields.at[:, :, pl.ds(y * quarter, quarter)], rows.at[:, pl.ds(y * block, block), :], local_sem.at[2]
    )
    load_quads = pltpu.make_async_copy(quads, quads_here, local_sem.at[3])
    load_pattern = pltpu.make_async_copy(pattern, pattern_here, local_sem.at[4])
    load_quads.start()
    load_pattern.start()
    load_basis.start()
    load_weight.start()
    load_own.start()

    with jax.named_scope("barrier"):
        barrier = pltpu.get_barrier_semaphore()
        for d in range(1, nz):
            pl.semaphore_signal(barrier, inc=1, device_id=at_z(turn(z, d, nz)), device_id_type=MESH)
        for d in range(1, NY):
            pl.semaphore_signal(barrier, inc=1, device_id=at_y(turn(y, d, NY)), device_id_type=MESH)
        for d in range(1, NX):
            other = at_cell(turn(x, d, NX) * CORES + core)
            pl.semaphore_signal(barrier, inc=1, device_id=other, device_id_type=MESH)
        pl.semaphore_signal(barrier, inc=1, device_id=sibling, device_id_type=MESH)
        pads = (NY * 2 - 1) * block
        rows[:, pads:, :] = jnp.zeros((3, rows.shape[1] - pads, quarter), jnp.bfloat16)
        load_quads.wait()
        load_pattern.wait()
        for pair in range(2):
            asked[y, z, pair : pair + 1, 0:here] = quads_here[2 * pair : 2 * pair + 1, :]
            asked[y, z, pair : pair + 1, here : 2 * here] = quads_here[2 * pair + 1 : 2 * pair + 2, :]
        used[y] = jnp.zeros(used.shape[1:], jnp.int32)
        used[y, 0:1, 0 : pattern.shape[1]] = pattern_here[...]
        pl.semaphore_wait(barrier, NY - 1 + nz - 1 + NX - 1 + CORES - 1)

    ask_copies = []
    for d in range(1, NY):
        ask_copies.append(
            remote(asked.at[y, z], asked.at[y, z], ask_send.at[d], ask_y.at[d], at_y(turn(y, d, NY)))
        )
        ask_copies[-1].start()
    use_copies = []
    for d in range(1, NY):
        use_copies.append(remote(used.at[y], used.at[y], use_send.at[d], use_recv.at[d], at_y(turn(y, d, NY))))
        use_copies[-1].start()

    def y_copy(c, d):
        target = turn(y, d, NY)
        return remote(
            fields.at[:, :, pl.ds(target * quarter + c * width, width)],
            rows.at[:, pl.ds(y * block, block), pl.ds(c * width, width)],
            fy_send.at[c, d],
            fy_recv.at[c, d],
            at_y(target),
        )

    above = at_z(turn(z, nz - 1, nz))

    def z_own(c):
        return remote(
            fields.at[:, :, pl.ds(y * quarter + c * width, width)],
            rows.at[:, pl.ds((NY + y) * block, block), pl.ds(c * width, width)],
            fz_send.at[c, y],
            fz_recv.at[c, y],
            above,
        )

    def z_pass(c, b):
        return remote(
            rows.at[:, pl.ds(b * block, block), pl.ds(c * width, width)],
            rows.at[:, pl.ds((NY + b) * block, block), pl.ds(c * width, width)],
            fz_send.at[c, b],
            fz_recv.at[c, b],
            above,
        )

    def start_own(c):
        @pl.when(y < NY - 1)
        def _():
            z_own(c).start()

        for d in (2, 1, 3):
            y_copy(c, d).start()

    for c in range(ahead):
        start_own(c)

    with jax.named_scope("ask"):
        for d in range(1, NY):
            ask_copies[d - 1].wait_recv()
        for d in range(1, nz):
            ask_copies.append(
                remote(asked.at[:, z], asked.at[:, z], ask_z_send.at[d], ask_z.at[d], at_z(turn(z, d, nz)))
            )
            ask_copies[-1].start()

    def forward(c):
        with jax.named_scope("forward"):
            for d in (1, 3, 2):
                y_copy(c, d).wait_recv()
                source = turn(y, NY - d, NY)

                @pl.when(source < NY - 1)
                def _(c=c, source=source):
                    z_pass(c, source).start()

            if c + ahead < chunks:
                start_own(c + ahead)

    load_own.wait()
    for c in range(early):
        forward(c)

    lanes = asked.shape[-1]
    earlier = (
        lax.broadcasted_iota(jnp.int32, (lanes, lanes), 0) < lax.broadcasted_iota(jnp.int32, (lanes, lanes), 1)
    ).astype(jnp.bfloat16)

    def slot_match(in_block, slot):
        before = jnp.dot(in_block.astype(jnp.bfloat16), earlier, preferred_element_type=jnp.float32)
        return jnp.logical_and(in_block > 0.5, before == slot.astype(jnp.float32))

    with jax.named_scope("onehot"):
        for d in range(1, nz):
            ask_copies[NY - 1 + d - 1].wait_recv()
        devices = NY * nz
        group = NY * slots

        first_half = lax.broadcasted_iota(jnp.int32, (devices, lanes), 1) < here

        def wide(row):
            line = asked[:, :, row // 2, :].reshape(devices, lanes)
            if row % 2:
                line = pltpu.roll(line, lanes - here, 1)
            line = jnp.where(first_half, line, -1).reshape(devices, 1, lanes)
            return jnp.broadcast_to(line, (devices, group, lanes))

        inner = lax.broadcasted_iota(jnp.int32, (devices, group, lanes), 1)
        a_wide = wide(0)
        in_block = jnp.where(lax.shift_right_arithmetic(a_wide, 4) == z * NY + lax.div(inner, slots), 1.0, 0.0)
        in_block = in_block.reshape(half, lanes)
        slot = lax.rem(inner, slots).reshape(half, lanes)
        match = slot_match(in_block, slot)
        lane = lax.broadcasted_iota(jnp.int32, (half, lanes), 1)

        def local(row):
            value = (wide(row) - (z * NY * block - 1)).reshape(half, lanes).astype(jnp.float32)
            return jnp.sum(jnp.where(match, value, 0.0), axis=1, keepdims=True)

        a, b, m, n = (local(row).astype(jnp.int32) for row in range(4))
        offset = lax.shift_right_arithmetic(m - 1, 4) - lax.shift_right_arithmetic(a - 1, 4)
        for d in range(1, NY):
            use_copies[d - 1].wait_recv()
        tiles = used[:, 0, :].reshape(NY, 1, lanes)
        tiles = jnp.broadcast_to(tiles, (NY, slots, lanes)).reshape(1, group, lanes)
        tiles = jnp.broadcast_to(tiles, (devices, group, lanes)).reshape(half, lanes)
        live = jnp.sum(jnp.where(lane == offset, tiles.astype(jnp.float32), 0.0), axis=1, keepdims=True)
        one = jnp.where(lane == a - 1, 1.0, 0.0) - jnp.where(lane == b - 1, 1.0, 0.0)
        onehot[0] = (live * one).astype(jnp.bfloat16).reshape(onehot.shape[1:])
        two = jnp.where(lane == m - 1, 1.0, 0.0) - jnp.where(lane == n - 1, 1.0, 0.0)
        onehot[1] = two.astype(jnp.bfloat16).reshape(onehot.shape[1:])

        slot_row = lax.broadcasted_iota(jnp.int32, (lane_group, lanes), 0)
        own_a = jnp.where(first_half[0:1], asked[y, z, 0:1, :], -1)
        own_a = jnp.broadcast_to(lax.shift_right_arithmetic(own_a, 4), (lane_group, lanes))
        own_block = jnp.where(own_a == lax.div(slot_row, slots), 1.0, 0.0)
        own_match = slot_match(own_block, lax.rem(slot_row, slots)).astype(jnp.float32)
        pick[...] = own_match.T[:here].astype(jnp.bfloat16)
        load_basis.wait()
        load_weight.wait()

    def gather(c):
        with jax.named_scope("gather_fields"):
            for b in range(NY - 1):
                z_pass(c, b).wait_recv()

    def project(c, sources, sinks):
        span = slice(c * width, (c + 1) * width)
        total = None
        for component in range(3):
            field = rows[component, :, span]
            left = jnp.dot(sources, field, preferred_element_type=jnp.float32)
            right = jnp.dot(sinks, field, preferred_element_type=jnp.float32)
            term = left * right
            total = term if total is None else total + term
        sensitivity = total * weight_here[:, span]
        high = sensitivity.astype(jnp.bfloat16)
        low = (sensitivity - high.astype(jnp.float32)).astype(jnp.bfloat16)
        part = jnp.dot(high, basis_here[span, :], preferred_element_type=jnp.float32)
        return part + jnp.dot(low, basis_here[span, :], preferred_element_type=jnp.float32)

    for c in range(chunks - 1):
        if c + early < chunks:
            forward(c + early)
        gather(c)
        with jax.named_scope("sensitivity"):
            part = project(c, onehot[0].reshape(half, lanes), onehot[1].reshape(half, lanes))
            part = part.reshape(partial.shape)
            partial[...] = part if c == 0 else partial[...] + part

    def own_half(other):
        return pl.ds(pl.multiple_of(other * (rank // CORES), 128), rank // CORES)

    def core_copy(d):
        target = turn(y, d, NY)
        return remote(
            partial.at[target, :, own_half(1 - core)],
            from_core.at[target],
            core_send.at[d],
            core_recv.at[d],
            sibling,
        )

    def y_sum_copy(d):
        target = turn(y, d, NY)
        return remote(to_y.at[target], from_y.at[d], y_send.at[d], y_recv.at[d], at_y(target))

    def sum_cores(d):
        target = turn(y, d, NY)
        core_copy(d).wait_recv()
        summed = partial[target, :, own_half(core)] + from_core[target]
        if d:
            to_y[target] = summed.astype(jnp.bfloat16)
            y_sum_copy(d).start()
        else:
            own_sum[...] = summed

    gather(chunks - 1)
    before = None
    for d in (2, 1, 3, 0):
        with jax.named_scope("last_chunk"):
            target = turn(y, d, NY)
            partial[target] = partial[target] + project(chunks - 1, onehot[0, target], onehot[1, target])
            core_copy(d).start()
        if before is not None:
            sum_cores(before)
        before = d
    sum_cores(before)

    with jax.named_scope("sum_y"):
        total = own_sum[...]
        for d in (1, 3, 2):
            y_sum_copy(d).wait_recv()
            total = total + from_y[d].astype(jnp.float32)

    def z_copy(d):
        target = turn(z, d, nz)
        return remote(to_z.at[target], from_z.at[z], z_send.at[d], z_recv.at[d], at_z(target))

    with jax.named_scope("return_z"):
        to_z[...] = total.astype(jnp.bfloat16).reshape(to_z.shape)
        for d in (4, 3, 5, 2, 6, 1, 7):
            if d < nz:
                z_copy(d).start()
        from_z[z] = to_z[z]
        for d in range(1, nz):
            z_copy(d).wait_recv()
        returned = from_z[...].reshape(lane_group, rank // CORES)
        mine[...] = jnp.dot(pick[...], returned, preferred_element_type=jnp.float32).astype(jnp.bfloat16)

    def x_copy(d):
        target = turn(x, d, NX)
        return remote(mine, from_x.at[d], x_send.at[d], x_recv.at[d], at_cell(target * CORES + core))

    with jax.named_scope("sum_x"):
        for d in (2, 1, 3):
            x_copy(d).start()
        total = mine[...].astype(jnp.float32)
        for d in (1, 3, 2):
            x_copy(d).wait_recv()
            total = total + from_x[d].astype(jnp.float32)
        total = jnp.concatenate([total, jnp.zeros((lanes - here, rank // CORES), jnp.float32)], axis=0).T
        turned[...] = total
        own_energy[...] = jnp.broadcast_to(jnp.sum(total * total, axis=0, keepdims=True), own_energy.shape)

    part = rank // (NX * CORES)
    chip_rows = lax.rem(x * CORES * part, rank // CORES)
    last = [
        remote(
            turned.at[pl.ds(pl.multiple_of(chip_rows + (1 - core) * part, 8), part)],
            from_sibling,
            last_send.at[0],
            last_recv.at[0],
            sibling,
        ),
        remote(own_energy, sibling_energy, last_send.at[1], last_recv.at[1], sibling),
    ]
    with jax.named_scope("cores"):
        for copy in last:
            copy.start()
        for copy in last:
            copy.wait_recv()
        kept = turned[pl.ds(pl.multiple_of(chip_rows + core * part, 8), part)]
        holder = lax.div(x * CORES * part, rank // CORES)
        chosen = jnp.where(holder == core, kept, from_sibling[...])
        projection[...] = chosen[:, :here]
        energy[...] = (own_energy[...] + sibling_energy[...])[0:1, :here]

    with jax.named_scope("drain"):
        for copy in ask_copies + use_copies:
            copy.wait_send()
        for c in range(chunks):
            for d in range(1, NY):
                y_copy(c, d).wait_send()
            for b in range(NY - 1):
                z_pass(c, b).wait_send()
        for d in range(NY):
            core_copy(d).wait_send()
        for d in range(1, NY):
            y_sum_copy(d).wait_send()
        for d in range(1, nz):
            z_copy(d).wait_send()
        for d in range(1, NX):
            x_copy(d).wait_send()
        for copy in last:
            copy.wait_send()


def per_device(fields, cell_weight, resolution_basis, pattern, quadrupoles, chunks=4, ahead=4, early=3):
    block, components, cells = fields.shape
    rank = resolution_basis.shape[1]
    here = quadrupoles.shape[0]
    nz = lax.axis_size("elec") // NY
    quarter = cells // NY
    part = rank // (NX * CORES)
    lanes = 128
    slots = CAP
    half = nz * NY * NY * slots
    group = nz * NY * slots
    held = 2 * NY * block
    dma = pltpu.SemaphoreType.DMA
    vmem = pl.BlockSpec(memory_space=pltpu.VMEM)
    anywhere = pl.BlockSpec(memory_space=pl.ANY)
    sizes = (nz, block, cells, chunks, ahead, early, slots, rank, here)
    projection, energy = pl.pallas_call(
        functools.partial(kernel, sizes),
        out_shape=(
            jax.ShapeDtypeStruct((part, here), jnp.float32),
            jax.ShapeDtypeStruct((1, here), jnp.float32),
        ),
        in_specs=[anywhere] * 5,
        out_specs=(vmem, vmem),
        scratch_shapes=[
            pltpu.VMEM((components, held, quarter), jnp.bfloat16),
            pltpu.VMEM((quarter, rank), jnp.bfloat16),
            pltpu.VMEM((1, quarter), jnp.float32),
            pltpu.VMEM((NY, nz, 2, lanes), jnp.int32),
            pltpu.VMEM((NY, 8, lanes), jnp.int32),
            pltpu.VMEM((2, NY, group, lanes), jnp.bfloat16),
            pltpu.VMEM((here, group), jnp.bfloat16),
            pltpu.VMEM((NY, group, rank), jnp.float32),
            pltpu.VMEM((NY, group, rank // CORES), jnp.float32),
            pltpu.VMEM((group, rank // CORES), jnp.float32),
            pltpu.VMEM((NY, group, rank // CORES), jnp.bfloat16),
            pltpu.VMEM((NY, group, rank // CORES), jnp.bfloat16),
            pltpu.VMEM((nz, NY * slots, rank // CORES), jnp.bfloat16),
            pltpu.VMEM((nz, NY * slots, rank // CORES), jnp.bfloat16),
            pltpu.VMEM((here, rank // CORES), jnp.bfloat16),
            pltpu.VMEM((NX, here, rank // CORES), jnp.bfloat16),
            pltpu.VMEM((rank // CORES, lanes), jnp.float32),
            pltpu.VMEM((part, lanes), jnp.float32),
            pltpu.VMEM((8, lanes), jnp.float32),
            pltpu.VMEM((8, lanes), jnp.float32),
            pltpu.VMEM((1, pattern.shape[1]), jnp.int32),
            pltpu.VMEM((4, here), jnp.int32),
            dma((5,)),
            dma((NY,)),
            dma((NY,)),
            dma((NY,)),
            dma((NY,)),
            dma((nz,)),
            dma((nz,)),
            dma((chunks, NY)),
            dma((chunks, NY)),
            dma((chunks, NY)),
            dma((chunks, NY)),
            dma((NX,)),
            dma((NX,)),
            dma((NX,)),
            dma((NX,)),
            dma((NY,)),
            dma((NY,)),
            dma((nz,)),
            dma((nz,)),
            dma((2,)),
            dma((2,)),
        ],
        compiler_params=pltpu.CompilerParams(
            collective_id=0, has_side_effects=True, vmem_limit_bytes=60 * 1024 * 1024
        ),
    )(
        fields.transpose(1, 0, 2),
        cell_weight.reshape(1, cells),
        resolution_basis,
        pattern,
        quadrupoles.T,
    )
    return projection, jnp.log1p(energy.reshape(here) / rank)


def solution(mesh):
    placed = (P("elec", None, "cell"), P("cell"), P("cell", None), P("elec", None), P("elec", None))
    return jax.shard_map(
        per_device,
        mesh=mesh,
        in_specs=placed,
        out_specs=(P("cell", "elec"), P("elec")),
        check_vma=False,
    )
```

```python
import functools

import jax
import jax.numpy as jnp
from jax import lax
from jax.experimental import pallas as pl
from jax.experimental.pallas import tpu as pltpu
from jax.sharding import PartitionSpec as P

NY = 4
NX = 4
CORES = 2
CAP = 4
MESH = pl.DeviceIdType.MESH


def kernel(
    sizes,
    fields,
    weight,
    basis,
    pattern,
    quads,
    projection,
    energy,
    rows,
    basis_here,
    weight_here,
    asked,
    used,
    onehot,
    pick,
    partial,
    from_core,
    own_sum,
    to_y,
    from_y,
    to_z,
    from_z,
    mine,
    from_x,
    turned,
    from_sibling,
    own_energy,
    sibling_energy,
    pattern_here,
    quads_here,
    local_sem,
    use_send,
    use_recv,
    ask_send,
    ask_y,
    ask_z_send,
    ask_z,
    fy_send,
    fy_recv,
    fz_send,
    fz_recv,
    core_send,
    core_recv,
    x_send,
    x_recv,
    y_send,
    y_recv,
    z_send,
    z_recv,
    last_send,
    last_recv,
):
    nz, block, cells, chunks, ahead, early, slots, rank, here = sizes
    quarter = cells // NY
    width = quarter // chunks
    lane_group = nz * NY * slots
    half = NY * lane_group
    elec = lax.axis_index("elec")
    cell = lax.axis_index("cell")
    z, y = lax.div(elec, NY), lax.rem(elec, NY)
    x, core = lax.div(cell, CORES), lax.rem(cell, CORES)

    def turn(value, step, size):
        return lax.rem(value + step, size)

    def at_y(other):
        return (z * NY + other, cell)

    def at_z(other):
        return (other * NY + y, cell)

    def at_cell(other):
        return (elec, other)

    sibling = at_cell(x * CORES + (1 - core))

    def remote(src, dst, send, recv, device):
        return pltpu.make_async_remote_copy(
            src_ref=src, dst_ref=dst, send_sem=send, recv_sem=recv, device_id=device, device_id_type=MESH
        )

    load_basis = pltpu.make_async_copy(basis.at[pl.ds(y * quarter, quarter)], basis_here, local_sem.at[0])
    load_weight = pltpu.make_async_copy(weight.at[:, pl.ds(y * quarter, quarter)], weight_here, local_sem.at[1])
    load_own = pltpu.make_async_copy(
        fields.at[:, :, pl.ds(y * quarter, quarter)], rows.at[:, pl.ds((1 + y) * block, block), :], local_sem.at[2]
    )
    load_quads = pltpu.make_async_copy(quads, quads_here, local_sem.at[3])
    load_pattern = pltpu.make_async_copy(pattern, pattern_here, local_sem.at[4])
    load_quads.start()
    load_pattern.start()
    load_basis.start()
    load_weight.start()
    load_own.start()

    with jax.named_scope("barrier"):
        barrier = pltpu.get_barrier_semaphore()
        for d in range(1, nz):
            pl.semaphore_signal(barrier, inc=1, device_id=at_z(turn(z, d, nz)), device_id_type=MESH)
        for d in range(1, NY):
            pl.semaphore_signal(barrier, inc=1, device_id=at_y(turn(y, d, NY)), device_id_type=MESH)
        for d in range(1, NX):
            other = at_cell(turn(x, d, NX) * CORES + core)
            pl.semaphore_signal(barrier, inc=1, device_id=other, device_id_type=MESH)
        pl.semaphore_signal(barrier, inc=1, device_id=sibling, device_id_type=MESH)
        pads = (NY * 2 - 1) * block
        rows[:, pads:, :] = jnp.zeros((3, rows.shape[1] - pads, quarter), jnp.bfloat16)
        load_quads.wait()
        load_pattern.wait()
        for pair in range(2):
            asked[y, z, pair : pair + 1, 0:here] = quads_here[2 * pair : 2 * pair + 1, :]
            asked[y, z, pair : pair + 1, here : 2 * here] = quads_here[2 * pair + 1 : 2 * pair + 2, :]
        used[y] = jnp.zeros(used.shape[1:], jnp.int32)
        used[y, 0:1, 0 : pattern.shape[1]] = pattern_here[...]
        pl.semaphore_wait(barrier, NY - 1 + nz - 1 + NX - 1 + CORES - 1)

    ask_copies = []
    for d in range(1, NY):
        ask_copies.append(
            remote(asked.at[y, z], asked.at[y, z], ask_send.at[d], ask_y.at[d], at_y(turn(y, d, NY)))
        )
        ask_copies[-1].start()
    use_copies = []
    for d in range(1, NY):
        use_copies.append(remote(used.at[y], used.at[y], use_send.at[d], use_recv.at[d], at_y(turn(y, d, NY))))
        use_copies[-1].start()

    def y_copy(c, d):
        target = turn(y, d, NY)
        return remote(
            fields.at[:, :, pl.ds(target * quarter + c * width, width)],
            rows.at[:, pl.ds((1 + y) * block, block), pl.ds(c * width, width)],
            fy_send.at[c, d],
            fy_recv.at[c, d],
            at_y(target),
        )

    above, below = at_z(turn(z, nz - 1, nz)), at_z(turn(z, 1, nz))
    passed = ((0, above, 1 + NY), (1, above, 2 + NY), (NY - 1, below, 0))

    def z_own(c, k):
        _, device, place = passed[k]
        return remote(
            fields.at[:, :, pl.ds(y * quarter + c * width, width)],
            rows.at[:, pl.ds(place * block, block), pl.ds(c * width, width)],
            fz_send.at[c, k],
            fz_recv.at[c, k],
            device,
        )

    def z_pass(c, k):
        b, device, place = passed[k]
        return remote(
            rows.at[:, pl.ds((1 + b) * block, block), pl.ds(c * width, width)],
            rows.at[:, pl.ds(place * block, block), pl.ds(c * width, width)],
            fz_send.at[c, k],
            fz_recv.at[c, k],
            device,
        )

    def start_own(c):
        for k, (b, _, _) in enumerate(passed):

            @pl.when(y == b)
            def _(k=k):
                z_own(c, k).start()

        for d in (2, 1, 3):
            y_copy(c, d).start()

    for c in range(ahead):
        start_own(c)

    with jax.named_scope("ask"):
        for d in range(1, NY):
            ask_copies[d - 1].wait_recv()
        for d in range(1, nz):
            ask_copies.append(
                remote(asked.at[:, z], asked.at[:, z], ask_z_send.at[d], ask_z.at[d], at_z(turn(z, d, nz)))
            )
            ask_copies[-1].start()
        for d in range(1, NY):
            use_copies[d - 1].wait_recv()
        use_copies.append(remote(used.at[NY - 1], used.at[NY], use_send.at[0], use_recv.at[0], below))
        use_copies[-1].start()

    def forward(c):
        with jax.named_scope("forward"):
            for d in (1, 3, 2):
                y_copy(c, d).wait_recv()
                source = turn(y, NY - d, NY)

                for k, (b, _, _) in enumerate(passed):

                    @pl.when(source == b)
                    def _(c=c, k=k):
                        z_pass(c, k).start()

            if c + ahead < chunks:
                start_own(c + ahead)

    load_own.wait()
    for c in range(early):
        forward(c)

    lanes = asked.shape[-1]
    earlier = (
        lax.broadcasted_iota(jnp.int32, (lanes, lanes), 0) < lax.broadcasted_iota(jnp.int32, (lanes, lanes), 1)
    ).astype(jnp.bfloat16)

    def slot_match(in_block, slot):
        before = jnp.dot(in_block.astype(jnp.bfloat16), earlier, preferred_element_type=jnp.float32)
        return jnp.logical_and(in_block > 0.5, before == slot.astype(jnp.float32))

    with jax.named_scope("onehot"):
        for d in range(1, nz):
            ask_copies[NY - 1 + d - 1].wait_recv()
        devices = NY * nz
        group = NY * slots

        blocks = NY * nz

        def source_of(a):
            return jnp.where(a < 0, -1, lax.rem(lax.shift_right_arithmetic(a, 4) + 1, blocks))

        first_half = lax.broadcasted_iota(jnp.int32, (devices, lanes), 1) < here

        def wide(row):
            line = asked[:, :, row // 2, :].reshape(devices, lanes)
            if row % 2:
                line = pltpu.roll(line, lanes - here, 1)
            line = jnp.where(first_half, line, -1).reshape(devices, 1, lanes)
            return jnp.broadcast_to(line, (devices, group, lanes))

        inner = lax.broadcasted_iota(jnp.int32, (devices, group, lanes), 1)
        in_block = jnp.where(source_of(wide(0)) == z * NY + lax.div(inner, slots), 1.0, 0.0)
        in_block = in_block.reshape(half, lanes)
        slot = lax.rem(inner, slots).reshape(half, lanes)
        match = slot_match(in_block, slot)
        lane = lax.broadcasted_iota(jnp.int32, (half, lanes), 1)

        def local(row):
            value = wide(row) - (z * NY - 1) * block
            value = jnp.where(value >= blocks * block, value - blocks * block, value) + 1
            value = value.reshape(half, lanes).astype(jnp.float32)
            return jnp.sum(jnp.where(match, value, 0.0), axis=1, keepdims=True)

        a, b, m, n = (local(row).astype(jnp.int32) for row in range(4))
        offset = lax.shift_right_arithmetic(m - 1, 4) - lax.shift_right_arithmetic(a - 1, 4)
        use_copies[-1].wait_recv()
        tiles = jnp.concatenate([used[NY, 0:1], used[0, 0:1], used[1, 0:1], used[2, 0:1]], axis=0)
        tiles = tiles.reshape(NY, 1, lanes)
        tiles = jnp.broadcast_to(tiles, (NY, slots, lanes)).reshape(1, group, lanes)
        tiles = jnp.broadcast_to(tiles, (devices, group, lanes)).reshape(half, lanes)
        live = jnp.sum(jnp.where(lane == offset, tiles.astype(jnp.float32), 0.0), axis=1, keepdims=True)
        one = jnp.where(lane == a - 1, 1.0, 0.0) - jnp.where(lane == b - 1, 1.0, 0.0)
        onehot[0] = (live * one).astype(jnp.bfloat16).reshape(onehot.shape[1:])
        two = jnp.where(lane == m - 1, 1.0, 0.0) - jnp.where(lane == n - 1, 1.0, 0.0)
        onehot[1] = two.astype(jnp.bfloat16).reshape(onehot.shape[1:])

        slot_row = lax.broadcasted_iota(jnp.int32, (lane_group, lanes), 0)
        own_a = jnp.where(first_half[0:1], asked[y, z, 0:1, :], -1)
        own_a = jnp.broadcast_to(source_of(own_a), (lane_group, lanes))
        own_block = jnp.where(own_a == lax.div(slot_row, slots), 1.0, 0.0)
        own_match = slot_match(own_block, lax.rem(slot_row, slots)).astype(jnp.float32)
        pick[...] = own_match.T[:here].astype(jnp.bfloat16)
        load_basis.wait()
        load_weight.wait()

    def gather(c):
        with jax.named_scope("gather_fields"):
            for k in range(len(passed)):
                z_pass(c, k).wait_recv()

    def project(c, sources, sinks):
        span = slice(c * width, (c + 1) * width)
        total = None
        for component in range(3):
            field = rows[component, :, span]
            left = jnp.dot(sources, field, preferred_element_type=jnp.float32)
            right = jnp.dot(sinks, field, preferred_element_type=jnp.float32)
            term = left * right
            total = term if total is None else total + term
        sensitivity = total * weight_here[:, span]
        high = sensitivity.astype(jnp.bfloat16)
        low = (sensitivity - high.astype(jnp.float32)).astype(jnp.bfloat16)
        part = jnp.dot(high, basis_here[span, :], preferred_element_type=jnp.float32)
        return part + jnp.dot(low, basis_here[span, :], preferred_element_type=jnp.float32)

    for c in range(chunks - 1):
        if c + early < chunks:
            forward(c + early)
        gather(c)
        with jax.named_scope("sensitivity"):
            part = project(c, onehot[0].reshape(half, lanes), onehot[1].reshape(half, lanes))
            part = part.reshape(partial.shape)
            partial[...] = part if c == 0 else partial[...] + part

    def own_half(other):
        return pl.ds(pl.multiple_of(other * (rank // CORES), 128), rank // CORES)

    def core_copy(d):
        target = turn(y, d, NY)
        return remote(
            partial.at[target, :, own_half(1 - core)],
            from_core.at[target],
            core_send.at[d],
            core_recv.at[d],
            sibling,
        )

    def y_sum_copy(d):
        target = turn(y, d, NY)
        return remote(to_y.at[target], from_y.at[d], y_send.at[d], y_recv.at[d], at_y(target))

    def sum_cores(d):
        target = turn(y, d, NY)
        core_copy(d).wait_recv()
        summed = partial[target, :, own_half(core)] + from_core[target]
        if d:
            to_y[target] = summed.astype(jnp.bfloat16)
            y_sum_copy(d).start()
        else:
            own_sum[...] = summed

    gather(chunks - 1)
    before = None
    for d in (2, 1, 3, 0):
        with jax.named_scope("last_chunk"):
            target = turn(y, d, NY)
            partial[target] = partial[target] + project(chunks - 1, onehot[0, target], onehot[1, target])
            core_copy(d).start()
        if before is not None:
            sum_cores(before)
        before = d
    sum_cores(before)

    with jax.named_scope("sum_y"):
        total = own_sum[...]
        for d in (1, 3, 2):
            y_sum_copy(d).wait_recv()
            total = total + from_y[d].astype(jnp.float32)

    def z_copy(d):
        target = turn(z, d, nz)
        return remote(to_z.at[target], from_z.at[z], z_send.at[d], z_recv.at[d], at_z(target))

    with jax.named_scope("return_z"):
        to_z[...] = total.astype(jnp.bfloat16).reshape(to_z.shape)
        for d in (4, 3, 5, 2, 6, 1, 7):
            if d < nz:
                z_copy(d).start()
        from_z[z] = to_z[z]
        for d in range(1, nz):
            z_copy(d).wait_recv()
        returned = from_z[...].reshape(lane_group, rank // CORES)
        mine[...] = jnp.dot(pick[...], returned, preferred_element_type=jnp.float32).astype(jnp.bfloat16)

    def x_copy(d):
        target = turn(x, d, NX)
        return remote(mine, from_x.at[d], x_send.at[d], x_recv.at[d], at_cell(target * CORES + core))

    with jax.named_scope("sum_x"):
        for d in (2, 1, 3):
            x_copy(d).start()
        total = mine[...].astype(jnp.float32)
        for d in (1, 3, 2):
            x_copy(d).wait_recv()
            total = total + from_x[d].astype(jnp.float32)
        total = jnp.concatenate([total, jnp.zeros((lanes - here, rank // CORES), jnp.float32)], axis=0).T
        turned[...] = total
        own_energy[...] = jnp.broadcast_to(jnp.sum(total * total, axis=0, keepdims=True), own_energy.shape)

    part = rank // (NX * CORES)
    chip_rows = lax.rem(x * CORES * part, rank // CORES)
    last = [
        remote(
            turned.at[pl.ds(pl.multiple_of(chip_rows + (1 - core) * part, 8), part)],
            from_sibling,
            last_send.at[0],
            last_recv.at[0],
            sibling,
        ),
        remote(own_energy, sibling_energy, last_send.at[1], last_recv.at[1], sibling),
    ]
    with jax.named_scope("cores"):
        for copy in last:
            copy.start()
        for copy in last:
            copy.wait_recv()
        kept = turned[pl.ds(pl.multiple_of(chip_rows + core * part, 8), part)]
        holder = lax.div(x * CORES * part, rank // CORES)
        chosen = jnp.where(holder == core, kept, from_sibling[...])
        projection[...] = chosen[:, :here]
        energy[...] = (own_energy[...] + sibling_energy[...])[0:1, :here]

    with jax.named_scope("drain"):
        for copy in ask_copies + use_copies:
            copy.wait_send()
        for c in range(chunks):
            for d in range(1, NY):
                y_copy(c, d).wait_send()
            for k in range(len(passed)):
                z_pass(c, k).wait_send()
        for d in range(NY):
            core_copy(d).wait_send()
        for d in range(1, NY):
            y_sum_copy(d).wait_send()
        for d in range(1, nz):
            z_copy(d).wait_send()
        for d in range(1, NX):
            x_copy(d).wait_send()
        for copy in last:
            copy.wait_send()


def per_device(fields, cell_weight, resolution_basis, pattern, quadrupoles, chunks=4, ahead=4, early=3):
    block, components, cells = fields.shape
    rank = resolution_basis.shape[1]
    here = quadrupoles.shape[0]
    nz = lax.axis_size("elec") // NY
    quarter = cells // NY
    part = rank // (NX * CORES)
    lanes = 128
    slots = CAP
    half = nz * NY * NY * slots
    group = nz * NY * slots
    held = 2 * NY * block
    dma = pltpu.SemaphoreType.DMA
    vmem = pl.BlockSpec(memory_space=pltpu.VMEM)
    anywhere = pl.BlockSpec(memory_space=pl.ANY)
    sizes = (nz, block, cells, chunks, ahead, early, slots, rank, here)
    projection, energy = pl.pallas_call(
        functools.partial(kernel, sizes),
        out_shape=(
            jax.ShapeDtypeStruct((part, here), jnp.float32),
            jax.ShapeDtypeStruct((1, here), jnp.float32),
        ),
        in_specs=[anywhere] * 5,
        out_specs=(vmem, vmem),
        scratch_shapes=[
            pltpu.VMEM((components, held, quarter), jnp.bfloat16),
            pltpu.VMEM((quarter, rank), jnp.bfloat16),
            pltpu.VMEM((1, quarter), jnp.float32),
            pltpu.VMEM((NY, nz, 2, lanes), jnp.int32),
            pltpu.VMEM((NY + 1, 8, lanes), jnp.int32),
            pltpu.VMEM((2, NY, group, lanes), jnp.bfloat16),
            pltpu.VMEM((here, group), jnp.bfloat16),
            pltpu.VMEM((NY, group, rank), jnp.float32),
            pltpu.VMEM((NY, group, rank // CORES), jnp.float32),
            pltpu.VMEM((group, rank // CORES), jnp.float32),
            pltpu.VMEM((NY, group, rank // CORES), jnp.bfloat16),
            pltpu.VMEM((NY, group, rank // CORES), jnp.bfloat16),
            pltpu.VMEM((nz, NY * slots, rank // CORES), jnp.bfloat16),
            pltpu.VMEM((nz, NY * slots, rank // CORES), jnp.bfloat16),
            pltpu.VMEM((here, rank // CORES), jnp.bfloat16),
            pltpu.VMEM((NX, here, rank // CORES), jnp.bfloat16),
            pltpu.VMEM((rank // CORES, lanes), jnp.float32),
            pltpu.VMEM((part, lanes), jnp.float32),
            pltpu.VMEM((8, lanes), jnp.float32),
            pltpu.VMEM((8, lanes), jnp.float32),
            pltpu.VMEM((1, pattern.shape[1]), jnp.int32),
            pltpu.VMEM((4, here), jnp.int32),
            dma((5,)),
            dma((NY,)),
            dma((NY,)),
            dma((NY,)),
            dma((NY,)),
            dma((nz,)),
            dma((nz,)),
            dma((chunks, NY)),
            dma((chunks, NY)),
            dma((chunks, NY)),
            dma((chunks, NY)),
            dma((NX,)),
            dma((NX,)),
            dma((NX,)),
            dma((NX,)),
            dma((NY,)),
            dma((NY,)),
            dma((nz,)),
            dma((nz,)),
            dma((2,)),
            dma((2,)),
        ],
        compiler_params=pltpu.CompilerParams(
            collective_id=0, has_side_effects=True, vmem_limit_bytes=60 * 1024 * 1024
        ),
    )(
        fields.transpose(1, 0, 2),
        cell_weight.reshape(1, cells),
        resolution_basis,
        pattern,
        quadrupoles.T,
    )
    return projection, jnp.log1p(energy.reshape(here) / rank)


def solution(mesh):
    placed = (P("elec", None, "cell"), P("cell"), P("cell", None), P("elec", None), P("elec", None))
    return jax.shard_map(
        per_device,
        mesh=mesh,
        in_specs=placed,
        out_specs=(P("cell", "elec"), P("elec")),
        check_vma=False,
    )
```

```python
import functools

import jax
import jax.numpy as jnp
from jax import lax
from jax.experimental import pallas as pl
from jax.experimental.pallas import tpu as pltpu
from jax.sharding import PartitionSpec as P

NY = 4
NX = 4
CORES = 2
CAP = 4
MESH = pl.DeviceIdType.MESH


def kernel(
    sizes,
    fields,
    weight,
    basis,
    pattern,
    quads,
    projection,
    energy,
    rows,
    basis_here,
    weight_here,
    own_fields,
    asked,
    used,
    onehot,
    pick,
    partial,
    from_core,
    own_sum,
    to_y,
    from_y,
    to_z,
    from_z,
    mine,
    from_x,
    turned,
    from_sibling,
    own_energy,
    sibling_energy,
    pattern_here,
    quads_here,
    local_sem,
    use_send,
    use_recv,
    ask_send,
    ask_y,
    ask_z_send,
    ask_z,
    fy_send,
    fy_recv,
    fz_send,
    fz_recv,
    core_send,
    core_recv,
    x_send,
    x_recv,
    y_send,
    y_recv,
    z_send,
    z_recv,
    last_send,
    last_recv,
):
    nz, block, cells, parts, ahead, early, slots, rank, here = sizes
    quarter = cells // NY
    shares = [quarter * share // sum(parts) for share in parts]
    chunks = len(parts)
    starts = [sum(shares[:c]) for c in range(chunks)]
    lane_group = nz * NY * slots
    half = NY * lane_group
    elec = lax.axis_index("elec")
    cell = lax.axis_index("cell")
    z, y = lax.div(elec, NY), lax.rem(elec, NY)
    x, core = lax.div(cell, CORES), lax.rem(cell, CORES)

    def turn(value, step, size):
        return lax.rem(value + step, size)

    def at_y(other):
        return (z * NY + other, cell)

    def at_z(other):
        return (other * NY + y, cell)

    def at_cell(other):
        return (elec, other)

    sibling = at_cell(x * CORES + (1 - core))

    def remote(src, dst, send, recv, device):
        return pltpu.make_async_remote_copy(
            src_ref=src, dst_ref=dst, send_sem=send, recv_sem=recv, device_id=device, device_id_type=MESH
        )

    load_basis = pltpu.make_async_copy(basis.at[pl.ds(y * quarter, quarter)], basis_here, local_sem.at[0])
    load_weight = pltpu.make_async_copy(weight.at[:, pl.ds(y * quarter, quarter)], weight_here, local_sem.at[1])
    load_own = pltpu.make_async_copy(
        fields.at[:, :, pl.ds(y * quarter, quarter)], rows.at[:, pl.ds((1 + y) * block, block), :], local_sem.at[2]
    )
    load_quads = pltpu.make_async_copy(quads, quads_here, local_sem.at[3])
    load_pattern = pltpu.make_async_copy(pattern, pattern_here, local_sem.at[4])
    load_quads.start()
    load_pattern.start()
    load_fields = pltpu.make_async_copy(fields, own_fields, local_sem.at[5])
    load_fields.start()
    load_basis.start()
    load_weight.start()
    load_own.start()

    with jax.named_scope("barrier"):
        barrier = pltpu.get_barrier_semaphore()
        for d in range(1, nz):
            pl.semaphore_signal(barrier, inc=1, device_id=at_z(turn(z, d, nz)), device_id_type=MESH)
        for d in range(1, NY):
            pl.semaphore_signal(barrier, inc=1, device_id=at_y(turn(y, d, NY)), device_id_type=MESH)
        for d in range(1, NX):
            other = at_cell(turn(x, d, NX) * CORES + core)
            pl.semaphore_signal(barrier, inc=1, device_id=other, device_id_type=MESH)
        pl.semaphore_signal(barrier, inc=1, device_id=sibling, device_id_type=MESH)
        pads = (NY * 2 - 1) * block
        rows[:, pads:, :] = jnp.zeros((3, rows.shape[1] - pads, quarter), jnp.bfloat16)
        load_quads.wait()
        load_pattern.wait()
        for pair in range(2):
            asked[y, z, pair : pair + 1, 0:here] = quads_here[2 * pair : 2 * pair + 1, :]
            asked[y, z, pair : pair + 1, here : 2 * here] = quads_here[2 * pair + 1 : 2 * pair + 2, :]
        used[y] = jnp.zeros(used.shape[1:], jnp.int32)
        used[y, 0:1, 0 : pattern.shape[1]] = pattern_here[...]
        load_fields.wait()
        pl.semaphore_wait(barrier, NY - 1 + nz - 1 + NX - 1 + CORES - 1)

    ask_copies = []
    for d in range(1, NY):
        ask_copies.append(
            remote(asked.at[y, z], asked.at[y, z], ask_send.at[d], ask_y.at[d], at_y(turn(y, d, NY)))
        )
        ask_copies[-1].start()
    use_copies = []
    for d in range(1, NY):
        use_copies.append(remote(used.at[y], used.at[y], use_send.at[d], use_recv.at[d], at_y(turn(y, d, NY))))
        use_copies[-1].start()

    def y_copy(c, d):
        target = turn(y, d, NY)
        return remote(
            own_fields.at[:, :, pl.ds(target * quarter + starts[c], shares[c])],
            rows.at[:, pl.ds((1 + y) * block, block), pl.ds(starts[c], shares[c])],
            fy_send.at[c, d],
            fy_recv.at[c, d],
            at_y(target),
        )

    above, below = at_z(turn(z, nz - 1, nz)), at_z(turn(z, 1, nz))
    passed = ((0, above, 1 + NY), (1, above, 2 + NY), (NY - 1, below, 0))

    def z_own(c, k):
        _, device, place = passed[k]
        return remote(
            own_fields.at[:, :, pl.ds(y * quarter + starts[c], shares[c])],
            rows.at[:, pl.ds(place * block, block), pl.ds(starts[c], shares[c])],
            fz_send.at[c, k],
            fz_recv.at[c, k],
            device,
        )

    def z_pass(c, k):
        b, device, place = passed[k]
        return remote(
            rows.at[:, pl.ds((1 + b) * block, block), pl.ds(starts[c], shares[c])],
            rows.at[:, pl.ds(place * block, block), pl.ds(starts[c], shares[c])],
            fz_send.at[c, k],
            fz_recv.at[c, k],
            device,
        )

    def start_own(c):
        for k, (b, _, _) in enumerate(passed):

            @pl.when(y == b)
            def _(k=k):
                z_own(c, k).start()

        for d in (2, 1, 3):
            y_copy(c, d).start()

    for c in range(ahead):
        start_own(c)

    with jax.named_scope("ask"):
        for d in range(1, NY):
            ask_copies[d - 1].wait_recv()
        for d in range(1, nz):
            ask_copies.append(
                remote(asked.at[:, z], asked.at[:, z], ask_z_send.at[d], ask_z.at[d], at_z(turn(z, d, nz)))
            )
            ask_copies[-1].start()
        for d in range(1, NY):
            use_copies[d - 1].wait_recv()
        use_copies.append(remote(used.at[NY - 1], used.at[NY], use_send.at[0], use_recv.at[0], below))
        use_copies[-1].start()

    def forward(c):
        with jax.named_scope("forward"):
            for d in (1, 3, 2):
                y_copy(c, d).wait_recv()
                source = turn(y, NY - d, NY)

                for k, (b, _, _) in enumerate(passed):

                    @pl.when(source == b)
                    def _(c=c, k=k):
                        z_pass(c, k).start()

            if c + ahead < chunks:
                start_own(c + ahead)

    load_own.wait()
    for c in range(early):
        forward(c)

    lanes = asked.shape[-1]
    earlier = (
        lax.broadcasted_iota(jnp.int32, (lanes, lanes), 0) < lax.broadcasted_iota(jnp.int32, (lanes, lanes), 1)
    ).astype(jnp.bfloat16)

    def slot_match(in_block, slot):
        before = jnp.dot(in_block.astype(jnp.bfloat16), earlier, preferred_element_type=jnp.float32)
        return jnp.logical_and(in_block > 0.5, before == slot.astype(jnp.float32))

    with jax.named_scope("onehot"):
        for d in range(1, nz):
            ask_copies[NY - 1 + d - 1].wait_recv()
        devices = NY * nz
        group = NY * slots

        blocks = NY * nz

        def source_of(a):
            return jnp.where(a < 0, -1, lax.rem(lax.shift_right_arithmetic(a, 4) + 1, blocks))

        first_half = lax.broadcasted_iota(jnp.int32, (devices, lanes), 1) < here

        def wide(row):
            line = asked[:, :, row // 2, :].reshape(devices, lanes)
            if row % 2:
                line = pltpu.roll(line, lanes - here, 1)
            line = jnp.where(first_half, line, -1).reshape(devices, 1, lanes)
            return jnp.broadcast_to(line, (devices, group, lanes))

        inner = lax.broadcasted_iota(jnp.int32, (devices, group, lanes), 1)
        in_block = jnp.where(source_of(wide(0)) == z * NY + lax.div(inner, slots), 1.0, 0.0)
        in_block = in_block.reshape(half, lanes)
        slot = lax.rem(inner, slots).reshape(half, lanes)
        match = slot_match(in_block, slot)
        lane = lax.broadcasted_iota(jnp.int32, (half, lanes), 1)

        def local(row):
            value = wide(row) - (z * NY - 1) * block
            value = jnp.where(value >= blocks * block, value - blocks * block, value) + 1
            value = value.reshape(half, lanes).astype(jnp.float32)
            return jnp.sum(jnp.where(match, value, 0.0), axis=1, keepdims=True)

        a, b, m, n = (local(row).astype(jnp.int32) for row in range(4))
        offset = lax.shift_right_arithmetic(m - 1, 4) - lax.shift_right_arithmetic(a - 1, 4)
        use_copies[-1].wait_recv()
        tiles = jnp.concatenate([used[NY, 0:1], used[0, 0:1], used[1, 0:1], used[2, 0:1]], axis=0)
        tiles = tiles.reshape(NY, 1, lanes)
        tiles = jnp.broadcast_to(tiles, (NY, slots, lanes)).reshape(1, group, lanes)
        tiles = jnp.broadcast_to(tiles, (devices, group, lanes)).reshape(half, lanes)
        live = jnp.sum(jnp.where(lane == offset, tiles.astype(jnp.float32), 0.0), axis=1, keepdims=True)
        one = jnp.where(lane == a - 1, 1.0, 0.0) - jnp.where(lane == b - 1, 1.0, 0.0)
        onehot[0] = (live * one).astype(jnp.bfloat16).reshape(onehot.shape[1:])
        two = jnp.where(lane == m - 1, 1.0, 0.0) - jnp.where(lane == n - 1, 1.0, 0.0)
        onehot[1] = two.astype(jnp.bfloat16).reshape(onehot.shape[1:])

        slot_row = lax.broadcasted_iota(jnp.int32, (lane_group, lanes), 0)
        own_a = jnp.where(first_half[0:1], asked[y, z, 0:1, :], -1)
        own_a = jnp.broadcast_to(source_of(own_a), (lane_group, lanes))
        own_block = jnp.where(own_a == lax.div(slot_row, slots), 1.0, 0.0)
        own_match = slot_match(own_block, lax.rem(slot_row, slots)).astype(jnp.float32)
        pick[...] = own_match.T[:here].astype(jnp.bfloat16)
        load_basis.wait()
        load_weight.wait()

    def gather(c):
        with jax.named_scope("gather_fields"):
            for k in range(len(passed)):
                z_pass(c, k).wait_recv()

    def project(c, sources, sinks):
        span = slice(starts[c], starts[c] + shares[c])
        total = None
        for component in range(3):
            field = rows[component, :, span]
            left = jnp.dot(sources, field, preferred_element_type=jnp.float32)
            right = jnp.dot(sinks, field, preferred_element_type=jnp.float32)
            term = left * right
            total = term if total is None else total + term
        sensitivity = total * weight_here[:, span]
        high = sensitivity.astype(jnp.bfloat16)
        low = (sensitivity - high.astype(jnp.float32)).astype(jnp.bfloat16)
        part = jnp.dot(high, basis_here[span, :], preferred_element_type=jnp.float32)
        return part + jnp.dot(low, basis_here[span, :], preferred_element_type=jnp.float32)

    for c in range(chunks - 1):
        if c + early < chunks:
            forward(c + early)
        gather(c)
        with jax.named_scope("sensitivity"):
            part = project(c, onehot[0].reshape(half, lanes), onehot[1].reshape(half, lanes))
            part = part.reshape(partial.shape)
            partial[...] = part if c == 0 else partial[...] + part

    def own_half(other):
        return pl.ds(pl.multiple_of(other * (rank // CORES), 128), rank // CORES)

    def core_copy(d):
        target = turn(y, d, NY)
        return remote(
            partial.at[target, :, own_half(1 - core)],
            from_core.at[target],
            core_send.at[d],
            core_recv.at[d],
            sibling,
        )

    def y_sum_copy(d):
        target = turn(y, d, NY)
        return remote(to_y.at[target], from_y.at[d], y_send.at[d], y_recv.at[d], at_y(target))

    def sum_cores(d):
        target = turn(y, d, NY)
        core_copy(d).wait_recv()
        summed = partial[target, :, own_half(core)] + from_core[target]
        if d:
            to_y[target] = summed.astype(jnp.bfloat16)
            y_sum_copy(d).start()
        else:
            own_sum[...] = summed

    gather(chunks - 1)
    with jax.named_scope("last_chunk"):
        part = project(chunks - 1, onehot[0].reshape(half, lanes), onehot[1].reshape(half, lanes))
        partial[...] = partial[...] + part.reshape(partial.shape)
    for d in (2, 1, 3, 0):
        core_copy(d).start()
    for d in (2, 1, 3, 0):
        sum_cores(d)

    with jax.named_scope("sum_y"):
        total = own_sum[...]
        for d in (1, 3, 2):
            y_sum_copy(d).wait_recv()
            total = total + from_y[d].astype(jnp.float32)

    def z_copy(d):
        target = turn(z, d, nz)
        return remote(to_z.at[target], from_z.at[z], z_send.at[d], z_recv.at[d], at_z(target))

    with jax.named_scope("return_z"):
        to_z[...] = total.astype(jnp.bfloat16).reshape(to_z.shape)
        for d in (4, 3, 5, 2, 6, 1, 7):
            if d < nz:
                z_copy(d).start()
        from_z[z] = to_z[z]
        for d in range(1, nz):
            z_copy(d).wait_recv()
        returned = from_z[...].reshape(lane_group, rank // CORES)
        mine[...] = jnp.dot(pick[...], returned, preferred_element_type=jnp.float32).astype(jnp.bfloat16)

    def x_copy(d):
        target = turn(x, d, NX)
        return remote(mine, from_x.at[d], x_send.at[d], x_recv.at[d], at_cell(target * CORES + core))

    with jax.named_scope("sum_x"):
        for d in (2, 1, 3):
            x_copy(d).start()
        total = mine[...].astype(jnp.float32)
        for d in (1, 3, 2):
            x_copy(d).wait_recv()
            total = total + from_x[d].astype(jnp.float32)
        total = jnp.concatenate([total, jnp.zeros((lanes - here, rank // CORES), jnp.float32)], axis=0).T
        turned[...] = total
        own_energy[...] = jnp.broadcast_to(jnp.sum(total * total, axis=0, keepdims=True), own_energy.shape)

    part = rank // (NX * CORES)
    chip_rows = lax.rem(x * CORES * part, rank // CORES)
    last = [
        remote(
            turned.at[pl.ds(pl.multiple_of(chip_rows + (1 - core) * part, 8), part)],
            from_sibling,
            last_send.at[0],
            last_recv.at[0],
            sibling,
        ),
        remote(own_energy, sibling_energy, last_send.at[1], last_recv.at[1], sibling),
    ]
    with jax.named_scope("cores"):
        for copy in last:
            copy.start()
        for copy in last:
            copy.wait_recv()
        kept = turned[pl.ds(pl.multiple_of(chip_rows + core * part, 8), part)]
        holder = lax.div(x * CORES * part, rank // CORES)
        chosen = jnp.where(holder == core, kept, from_sibling[...])
        projection[...] = chosen[:, :here]
        energy[...] = (own_energy[...] + sibling_energy[...])[0:1, :here]

    with jax.named_scope("drain"):
        for copy in ask_copies + use_copies:
            copy.wait_send()
        for c in range(chunks):
            for d in range(1, NY):
                y_copy(c, d).wait_send()
            for k in range(len(passed)):
                z_pass(c, k).wait_send()
        for d in range(NY):
            core_copy(d).wait_send()
        for d in range(1, NY):
            y_sum_copy(d).wait_send()
        for d in range(1, nz):
            z_copy(d).wait_send()
        for d in range(1, NX):
            x_copy(d).wait_send()
        for copy in last:
            copy.wait_send()


def per_device(fields, cell_weight, resolution_basis, pattern, quadrupoles):
    block, components, cells = fields.shape
    parts = (1, 1, 1, 1)
    chunks = ahead = len(parts)
    early = chunks - 1
    rank = resolution_basis.shape[1]
    here = quadrupoles.shape[0]
    nz = lax.axis_size("elec") // NY
    quarter = cells // NY
    part = rank // (NX * CORES)
    lanes = 128
    slots = CAP
    half = nz * NY * NY * slots
    group = nz * NY * slots
    held = 2 * NY * block
    dma = pltpu.SemaphoreType.DMA
    vmem = pl.BlockSpec(memory_space=pltpu.VMEM)
    anywhere = pl.BlockSpec(memory_space=pl.ANY)
    sizes = (nz, block, cells, parts, ahead, early, slots, rank, here)
    projection, energy = pl.pallas_call(
        functools.partial(kernel, sizes),
        out_shape=(
            jax.ShapeDtypeStruct((part, here), jnp.float32),
            jax.ShapeDtypeStruct((1, here), jnp.float32),
        ),
        in_specs=[anywhere] * 5,
        out_specs=(vmem, vmem),
        scratch_shapes=[
            pltpu.VMEM((components, held, quarter), jnp.bfloat16),
            pltpu.VMEM((quarter, rank), jnp.bfloat16),
            pltpu.VMEM((1, quarter), jnp.float32),
            pltpu.VMEM((components, block, cells), jnp.bfloat16),
            pltpu.VMEM((NY, nz, 2, lanes), jnp.int32),
            pltpu.VMEM((NY + 1, 8, lanes), jnp.int32),
            pltpu.VMEM((2, NY, group, lanes), jnp.bfloat16),
            pltpu.VMEM((here, group), jnp.bfloat16),
            pltpu.VMEM((NY, group, rank), jnp.float32),
            pltpu.VMEM((NY, group, rank // CORES), jnp.float32),
            pltpu.VMEM((group, rank // CORES), jnp.float32),
            pltpu.VMEM((NY, group, rank // CORES), jnp.bfloat16),
            pltpu.VMEM((NY, group, rank // CORES), jnp.bfloat16),
            pltpu.VMEM((nz, NY * slots, rank // CORES), jnp.bfloat16),
            pltpu.VMEM((nz, NY * slots, rank // CORES), jnp.bfloat16),
            pltpu.VMEM((here, rank // CORES), jnp.bfloat16),
            pltpu.VMEM((NX, here, rank // CORES), jnp.bfloat16),
            pltpu.VMEM((rank // CORES, lanes), jnp.float32),
            pltpu.VMEM((part, lanes), jnp.float32),
            pltpu.VMEM((8, lanes), jnp.float32),
            pltpu.VMEM((8, lanes), jnp.float32),
            pltpu.VMEM((1, pattern.shape[1]), jnp.int32),
            pltpu.VMEM((4, here), jnp.int32),
            dma((6,)),
            dma((NY,)),
            dma((NY,)),
            dma((NY,)),
            dma((NY,)),
            dma((nz,)),
            dma((nz,)),
            dma((chunks, NY)),
            dma((chunks, NY)),
            dma((chunks, NY)),
            dma((chunks, NY)),
            dma((NX,)),
            dma((NX,)),
            dma((NX,)),
            dma((NX,)),
            dma((NY,)),
            dma((NY,)),
            dma((nz,)),
            dma((nz,)),
            dma((2,)),
            dma((2,)),
        ],
        compiler_params=pltpu.CompilerParams(
            collective_id=0, has_side_effects=True, vmem_limit_bytes=60 * 1024 * 1024
        ),
    )(
        fields.transpose(1, 0, 2),
        cell_weight.reshape(1, cells),
        resolution_basis,
        pattern,
        quadrupoles.T,
    )
    return projection, jnp.log1p(energy.reshape(here) / rank)


def solution(mesh):
    placed = (P("elec", None, "cell"), P("cell"), P("cell", None), P("elec", None), P("elec", None))
    return jax.shard_map(
        per_device,
        mesh=mesh,
        in_specs=placed,
        out_specs=(P("cell", "elec"), P("elec")),
        check_vma=False,
    )
```

```python
import functools

import jax
import jax.numpy as jnp
from jax import lax
from jax.experimental import pallas as pl
from jax.experimental.pallas import tpu as pltpu
from jax.sharding import PartitionSpec as P

NY = 4
NX = 4
CORES = 2
CAP = 4
MESH = pl.DeviceIdType.MESH


def kernel(
    sizes,
    fields,
    weight,
    basis,
    pattern,
    quads,
    projection,
    energy,
    rows,
    basis_here,
    weight_here,
    own_fields,
    asked,
    used,
    onehot,
    pick,
    partial,
    from_core,
    own_sum,
    to_y,
    from_y,
    to_z,
    from_z,
    mine,
    from_x,
    turned,
    from_sibling,
    own_energy,
    sibling_energy,
    pattern_here,
    quads_here,
    local_sem,
    use_send,
    use_recv,
    ask_send,
    ask_y,
    ask_z_send,
    ask_z,
    fy_send,
    fy_recv,
    fz_send,
    fz_recv,
    core_send,
    core_recv,
    x_send,
    x_recv,
    y_send,
    y_recv,
    z_send,
    z_recv,
    last_send,
    last_recv,
):
    nz, block, cells, parts, ahead, early, slots, rank, here = sizes
    quarter = cells // NY
    shares = [quarter * share // sum(parts) for share in parts]
    chunks = len(parts)
    starts = [sum(shares[:c]) for c in range(chunks)]
    lane_group = nz * NY * slots
    half = NY * lane_group
    elec = lax.axis_index("elec")
    cell = lax.axis_index("cell")
    z, y = lax.div(elec, NY), lax.rem(elec, NY)
    x, core = lax.div(cell, CORES), lax.rem(cell, CORES)

    def turn(value, step, size):
        return lax.rem(value + step, size)

    def at_y(other):
        return (z * NY + other, cell)

    def at_z(other):
        return (other * NY + y, cell)

    def at_cell(other):
        return (elec, other)

    sibling = at_cell(x * CORES + (1 - core))

    def remote(src, dst, send, recv, device):
        return pltpu.make_async_remote_copy(
            src_ref=src, dst_ref=dst, send_sem=send, recv_sem=recv, device_id=device, device_id_type=MESH
        )

    load_basis = pltpu.make_async_copy(basis.at[pl.ds(y * quarter, quarter)], basis_here, local_sem.at[0])
    load_weight = pltpu.make_async_copy(weight.at[:, pl.ds(y * quarter, quarter)], weight_here, local_sem.at[1])
    load_own = pltpu.make_async_copy(
        fields.at[:, :, pl.ds(y * quarter, quarter)], rows.at[:, pl.ds((1 + y) * block, block), :], local_sem.at[2]
    )
    load_quads = pltpu.make_async_copy(quads, quads_here, local_sem.at[3])
    load_pattern = pltpu.make_async_copy(pattern, pattern_here, local_sem.at[4])
    load_quads.start()
    load_pattern.start()
    load_fields = pltpu.make_async_copy(fields, own_fields, local_sem.at[5])
    load_fields.start()
    load_basis.start()
    load_weight.start()
    load_own.start()

    with jax.named_scope("barrier"):
        barrier = pltpu.get_barrier_semaphore()
        for d in range(1, nz):
            pl.semaphore_signal(barrier, inc=1, device_id=at_z(turn(z, d, nz)), device_id_type=MESH)
        for d in range(1, NY):
            pl.semaphore_signal(barrier, inc=1, device_id=at_y(turn(y, d, NY)), device_id_type=MESH)
        for d in range(1, NX):
            other = at_cell(turn(x, d, NX) * CORES + core)
            pl.semaphore_signal(barrier, inc=1, device_id=other, device_id_type=MESH)
        pl.semaphore_signal(barrier, inc=1, device_id=sibling, device_id_type=MESH)
        pads = (NY * 2 - 1) * block
        rows[:, pads:, :] = jnp.zeros((3, rows.shape[1] - pads, quarter), jnp.bfloat16)
        load_quads.wait()
        load_pattern.wait()
        for pair in range(2):
            asked[y, z, pair : pair + 1, 0:here] = quads_here[2 * pair : 2 * pair + 1, :]
            asked[y, z, pair : pair + 1, here : 2 * here] = quads_here[2 * pair + 1 : 2 * pair + 2, :]
        used[y] = jnp.zeros(used.shape[1:], jnp.int32)
        used[y, 0:1, 0 : pattern.shape[1]] = pattern_here[...]
        load_fields.wait()
        pl.semaphore_wait(barrier, NY - 1 + nz - 1 + NX - 1 + CORES - 1)

    ask_copies = []
    for d in range(1, NY):
        ask_copies.append(
            remote(asked.at[y, z], asked.at[y, z], ask_send.at[d], ask_y.at[d], at_y(turn(y, d, NY)))
        )
        ask_copies[-1].start()
    use_copies = []
    for d in range(1, NY):
        use_copies.append(remote(used.at[y], used.at[y], use_send.at[d], use_recv.at[d], at_y(turn(y, d, NY))))
        use_copies[-1].start()

    def y_copy(c, d):
        target = turn(y, d, NY)
        return remote(
            own_fields.at[:, :, pl.ds(target * quarter + starts[c], shares[c])],
            rows.at[:, pl.ds((1 + y) * block, block), pl.ds(starts[c], shares[c])],
            fy_send.at[c, d],
            fy_recv.at[c, d],
            at_y(target),
        )

    above, below = at_z(turn(z, nz - 1, nz)), at_z(turn(z, 1, nz))
    passed = ((0, above, 1 + NY), (1, above, 2 + NY), (NY - 1, below, 0))

    def z_own(c, k):
        _, device, place = passed[k]
        return remote(
            own_fields.at[:, :, pl.ds(y * quarter + starts[c], shares[c])],
            rows.at[:, pl.ds(place * block, block), pl.ds(starts[c], shares[c])],
            fz_send.at[c, k],
            fz_recv.at[c, k],
            device,
        )

    def z_pass(c, k):
        b, device, place = passed[k]
        return remote(
            rows.at[:, pl.ds((1 + b) * block, block), pl.ds(starts[c], shares[c])],
            rows.at[:, pl.ds(place * block, block), pl.ds(starts[c], shares[c])],
            fz_send.at[c, k],
            fz_recv.at[c, k],
            device,
        )

    def start_own(c):
        for k, (b, _, _) in enumerate(passed):

            @pl.when(y == b)
            def _(k=k):
                z_own(c, k).start()

        for d in (2, 1, 3):
            y_copy(c, d).start()

    for c in range(ahead):
        start_own(c)

    with jax.named_scope("ask"):
        for d in range(1, NY):
            ask_copies[d - 1].wait_recv()
        for d in range(1, nz):
            ask_copies.append(
                remote(asked.at[:, z], asked.at[:, z], ask_z_send.at[d], ask_z.at[d], at_z(turn(z, d, nz)))
            )
            ask_copies[-1].start()
        for d in range(1, NY):
            use_copies[d - 1].wait_recv()
        use_copies.append(remote(used.at[NY - 1], used.at[NY], use_send.at[0], use_recv.at[0], below))
        use_copies[-1].start()

    def forward(c):
        with jax.named_scope("forward"):
            for d in (1, 3, 2):
                y_copy(c, d).wait_recv()
                source = turn(y, NY - d, NY)

                for k, (b, _, _) in enumerate(passed):

                    @pl.when(source == b)
                    def _(c=c, k=k):
                        z_pass(c, k).start()

            if c + ahead < chunks:
                start_own(c + ahead)

    load_own.wait()
    for c in range(early):
        forward(c)

    lanes = asked.shape[-1]
    earlier = (
        lax.broadcasted_iota(jnp.int32, (lanes, lanes), 0) < lax.broadcasted_iota(jnp.int32, (lanes, lanes), 1)
    ).astype(jnp.bfloat16)

    def slot_match(in_block, slot):
        before = jnp.dot(in_block.astype(jnp.bfloat16), earlier, preferred_element_type=jnp.float32)
        return jnp.logical_and(in_block > 0.5, before == slot.astype(jnp.float32))

    with jax.named_scope("onehot"):
        for d in range(1, nz):
            ask_copies[NY - 1 + d - 1].wait_recv()
        devices = NY * nz
        group = NY * slots

        blocks = NY * nz

        def source_of(a):
            return jnp.where(a < 0, -1, lax.rem(lax.shift_right_arithmetic(a, 4) + 1, blocks))

        first_half = lax.broadcasted_iota(jnp.int32, (devices, lanes), 1) < here

        def wide(row):
            line = asked[:, :, row // 2, :].reshape(devices, lanes)
            if row % 2:
                line = pltpu.roll(line, lanes - here, 1)
            line = jnp.where(first_half, line, -1).reshape(devices, 1, lanes)
            return jnp.broadcast_to(line, (devices, group, lanes))

        inner = lax.broadcasted_iota(jnp.int32, (devices, group, lanes), 1)
        in_block = jnp.where(source_of(wide(0)) == z * NY + lax.div(inner, slots), 1.0, 0.0)
        in_block = in_block.reshape(half, lanes)
        slot = lax.rem(inner, slots).reshape(half, lanes)
        match = slot_match(in_block, slot)
        lane = lax.broadcasted_iota(jnp.int32, (half, lanes), 1)

        def local(row):
            value = wide(row) - (z * NY - 1) * block
            value = jnp.where(value >= blocks * block, value - blocks * block, value) + 1
            value = value.reshape(half, lanes).astype(jnp.float32)
            return jnp.sum(jnp.where(match, value, 0.0), axis=1, keepdims=True)

        a, b, m, n = (local(row).astype(jnp.int32) for row in range(4))
        offset = lax.shift_right_arithmetic(m - 1, 4) - lax.shift_right_arithmetic(a - 1, 4)
        use_copies[-1].wait_recv()
        tiles = jnp.concatenate([used[NY, 0:1], used[0, 0:1], used[1, 0:1], used[2, 0:1]], axis=0)
        tiles = tiles.reshape(NY, 1, lanes)
        tiles = jnp.broadcast_to(tiles, (NY, slots, lanes)).reshape(1, group, lanes)
        tiles = jnp.broadcast_to(tiles, (devices, group, lanes)).reshape(half, lanes)
        live = jnp.sum(jnp.where(lane == offset, tiles.astype(jnp.float32), 0.0), axis=1, keepdims=True)
        one = jnp.where(lane == a - 1, 1.0, 0.0) - jnp.where(lane == b - 1, 1.0, 0.0)
        onehot[0] = (live * one).astype(jnp.bfloat16).reshape(onehot.shape[1:])
        two = jnp.where(lane == m - 1, 1.0, 0.0) - jnp.where(lane == n - 1, 1.0, 0.0)
        onehot[1] = two.astype(jnp.bfloat16).reshape(onehot.shape[1:])

        slot_row = lax.broadcasted_iota(jnp.int32, (lane_group, lanes), 0)
        own_a = jnp.where(first_half[0:1], asked[y, z, 0:1, :], -1)
        own_a = jnp.broadcast_to(source_of(own_a), (lane_group, lanes))
        own_block = jnp.where(own_a == lax.div(slot_row, slots), 1.0, 0.0)
        own_match = slot_match(own_block, lax.rem(slot_row, slots)).astype(jnp.float32)
        pick[...] = own_match.T[:here].astype(jnp.bfloat16)
        load_basis.wait()
        load_weight.wait()

    def gather(c):
        with jax.named_scope("gather_fields"):
            for k in range(len(passed)):
                z_pass(c, k).wait_recv()

    def project(c, sources, sinks):
        span = slice(starts[c], starts[c] + shares[c])
        total = None
        for component in range(3):
            field = rows[component, :, span]
            left = jnp.dot(sources, field, preferred_element_type=jnp.float32)
            right = jnp.dot(sinks, field, preferred_element_type=jnp.float32)
            term = left * right
            total = term if total is None else total + term
        sensitivity = total * weight_here[:, span]
        high = sensitivity.astype(jnp.bfloat16)
        low = (sensitivity - high.astype(jnp.float32)).astype(jnp.bfloat16)
        part = jnp.dot(high, basis_here[span, :], preferred_element_type=jnp.float32)
        return part + jnp.dot(low, basis_here[span, :], preferred_element_type=jnp.float32)

    for c in range(chunks - 1):
        if c + early < chunks:
            forward(c + early)
        gather(c)
        with jax.named_scope("sensitivity"):
            part = project(c, onehot[0].reshape(half, lanes), onehot[1].reshape(half, lanes))
            part = part.reshape(partial.shape)
            partial[...] = part if c == 0 else partial[...] + part

    def own_half(other):
        return pl.ds(pl.multiple_of(other * (rank // CORES), 128), rank // CORES)

    def core_copy(d):
        target = turn(y, d, NY)
        return remote(
            partial.at[target, :, own_half(1 - core)],
            from_core.at[target],
            core_send.at[d],
            core_recv.at[d],
            sibling,
        )

    def y_sum_copy(d):
        target = turn(y, d, NY)
        return remote(to_y.at[target], from_y.at[d], y_send.at[d], y_recv.at[d], at_y(target))

    def sum_cores(d):
        target = turn(y, d, NY)
        core_copy(d).wait_recv()
        summed = partial[target, :, own_half(core)] + from_core[target]
        if d:
            to_y[target] = summed.astype(jnp.bfloat16)
            y_sum_copy(d).start()
        else:
            own_sum[...] = summed

    gather(chunks - 1)
    with jax.named_scope("last_chunk"):
        part = project(chunks - 1, onehot[0].reshape(half, lanes), onehot[1].reshape(half, lanes))
        partial[...] = partial[...] + part.reshape(partial.shape)
    for d in (2, 1, 3, 0):
        core_copy(d).start()
    for d in (2, 1, 3, 0):
        sum_cores(d)

    with jax.named_scope("sum_y"):
        total = own_sum[...]
        for d in (1, 3, 2):
            y_sum_copy(d).wait_recv()
            total = total + from_y[d].astype(jnp.float32)

    def z_copy(d):
        target = turn(z, d, nz)
        return remote(to_z.at[target], from_z.at[z], z_send.at[d], z_recv.at[d], at_z(target))

    with jax.named_scope("return_z"):
        to_z[...] = total.astype(jnp.bfloat16).reshape(to_z.shape)
        for d in (4, 3, 5, 2, 6, 1, 7):
            if d < nz:
                z_copy(d).start()
        from_z[z] = to_z[z]
        for d in range(1, nz):
            z_copy(d).wait_recv()
        returned = from_z[...].reshape(lane_group, rank // CORES)
        mine[...] = jnp.dot(pick[...], returned, preferred_element_type=jnp.float32).astype(jnp.bfloat16)

    def x_copy(d):
        target = turn(x, d, NX)
        return remote(mine, from_x.at[d], x_send.at[d], x_recv.at[d], at_cell(target * CORES + core))

    part = rank // (NX * CORES)
    chip_rows = lax.rem(x * CORES * part, rank // CORES)
    last = [
        remote(
            turned.at[pl.ds(pl.multiple_of(chip_rows + (1 - core) * part, 8), part)],
            from_sibling,
            last_send.at[0],
            last_recv.at[0],
            sibling,
        ),
        remote(own_energy, sibling_energy, last_send.at[1], last_recv.at[1], sibling),
    ]
    with jax.named_scope("sum_x"):
        for d in (2, 1, 3):
            x_copy(d).start()
        total = mine[...].astype(jnp.float32)
        for d in (1, 3, 2):
            x_copy(d).wait_recv()
            total = total + from_x[d].astype(jnp.float32)
        total = jnp.concatenate([total, jnp.zeros((lanes - here, rank // CORES), jnp.float32)], axis=0).T
        turned[...] = total
        last[0].start()
        own_energy[...] = jnp.broadcast_to(jnp.sum(total * total, axis=0, keepdims=True), own_energy.shape)

    with jax.named_scope("cores"):
        last[1].start()
        for copy in last:
            copy.wait_recv()
        kept = turned[pl.ds(pl.multiple_of(chip_rows + core * part, 8), part)]
        holder = lax.div(x * CORES * part, rank // CORES)
        chosen = jnp.where(holder == core, kept, from_sibling[...])
        projection[...] = chosen[:, :here]
        energy[...] = (own_energy[...] + sibling_energy[...])[0:1, :here]

    with jax.named_scope("drain"):
        for copy in ask_copies + use_copies:
            copy.wait_send()
        for c in range(chunks):
            for d in range(1, NY):
                y_copy(c, d).wait_send()
            for k in range(len(passed)):
                z_pass(c, k).wait_send()
        for d in range(NY):
            core_copy(d).wait_send()
        for d in range(1, NY):
            y_sum_copy(d).wait_send()
        for d in range(1, nz):
            z_copy(d).wait_send()
        for d in range(1, NX):
            x_copy(d).wait_send()
        for copy in last:
            copy.wait_send()


def per_device(fields, cell_weight, resolution_basis, pattern, quadrupoles):
    block, components, cells = fields.shape
    parts = (1, 1, 1, 1)
    chunks = ahead = len(parts)
    early = chunks - 1
    rank = resolution_basis.shape[1]
    here = quadrupoles.shape[0]
    nz = lax.axis_size("elec") // NY
    quarter = cells // NY
    part = rank // (NX * CORES)
    lanes = 128
    slots = CAP
    half = nz * NY * NY * slots
    group = nz * NY * slots
    held = 2 * NY * block
    dma = pltpu.SemaphoreType.DMA
    vmem = pl.BlockSpec(memory_space=pltpu.VMEM)
    anywhere = pl.BlockSpec(memory_space=pl.ANY)
    sizes = (nz, block, cells, parts, ahead, early, slots, rank, here)
    projection, energy = pl.pallas_call(
        functools.partial(kernel, sizes),
        out_shape=(
            jax.ShapeDtypeStruct((part, here), jnp.float32),
            jax.ShapeDtypeStruct((1, here), jnp.float32),
        ),
        in_specs=[anywhere] * 5,
        out_specs=(vmem, vmem),
        scratch_shapes=[
            pltpu.VMEM((components, held, quarter), jnp.bfloat16),
            pltpu.VMEM((quarter, rank), jnp.bfloat16),
            pltpu.VMEM((1, quarter), jnp.float32),
            pltpu.VMEM((components, block, cells), jnp.bfloat16),
            pltpu.VMEM((NY, nz, 2, lanes), jnp.int32),
            pltpu.VMEM((NY + 1, 8, lanes), jnp.int32),
            pltpu.VMEM((2, NY, group, lanes), jnp.bfloat16),
            pltpu.VMEM((here, group), jnp.bfloat16),
            pltpu.VMEM((NY, group, rank), jnp.float32),
            pltpu.VMEM((NY, group, rank // CORES), jnp.float32),
            pltpu.VMEM((group, rank // CORES), jnp.float32),
            pltpu.VMEM((NY, group, rank // CORES), jnp.bfloat16),
            pltpu.VMEM((NY, group, rank // CORES), jnp.bfloat16),
            pltpu.VMEM((nz, NY * slots, rank // CORES), jnp.bfloat16),
            pltpu.VMEM((nz, NY * slots, rank // CORES), jnp.bfloat16),
            pltpu.VMEM((here, rank // CORES), jnp.bfloat16),
            pltpu.VMEM((NX, here, rank // CORES), jnp.bfloat16),
            pltpu.VMEM((rank // CORES, lanes), jnp.float32),
            pltpu.VMEM((part, lanes), jnp.float32),
            pltpu.VMEM((8, lanes), jnp.float32),
            pltpu.VMEM((8, lanes), jnp.float32),
            pltpu.VMEM((1, pattern.shape[1]), jnp.int32),
            pltpu.VMEM((4, here), jnp.int32),
            dma((6,)),
            dma((NY,)),
            dma((NY,)),
            dma((NY,)),
            dma((NY,)),
            dma((nz,)),
            dma((nz,)),
            dma((chunks, NY)),
            dma((chunks, NY)),
            dma((chunks, NY)),
            dma((chunks, NY)),
            dma((NX,)),
            dma((NX,)),
            dma((NX,)),
            dma((NX,)),
            dma((NY,)),
            dma((NY,)),
            dma((nz,)),
            dma((nz,)),
            dma((2,)),
            dma((2,)),
        ],
        compiler_params=pltpu.CompilerParams(
            collective_id=0, has_side_effects=True, vmem_limit_bytes=60 * 1024 * 1024
        ),
    )(
        fields.transpose(1, 0, 2),
        cell_weight.reshape(1, cells),
        resolution_basis,
        pattern,
        quadrupoles.T,
    )
    return projection, jnp.log1p(energy.reshape(here) / rank)


def solution(mesh):
    placed = (P("elec", None, "cell"), P("cell"), P("cell", None), P("elec", None), P("elec", None))
    return jax.shard_map(
        per_device,
        mesh=mesh,
        in_specs=placed,
        out_specs=(P("cell", "elec"), P("elec")),
        check_vma=False,
    )
```
